128 devices in a mesh: band: 4 (over z), region: 32 (over y, x, core).
Axes of the slice: x: 4, y: 4, z: 4, core: 2. Of those that a mesh axis runs over, the one named last changes fastest.
Arguments:
- grid_latent: bfloat16 [131072, 512], P(('band', 'region')), may hold values from -6 to 6
- mesh_latent: bfloat16 [8192, 512], P('region'), may hold values from -6 to 6
- encode_sender: int32 [819200], P(('band', 'region')), may hold values from 0 to 1023
- encode_receiver: int32 [819200], P(('band', 'region')), may hold values from 0 to 255
- encode_live: int32 [128, 35], P(('band', 'region')), may hold values from 1 to 2048, as said below
- encode_feature: float32 [4, 819200], P(None, ('band', 'region')), may hold values from -6 to 6
- mesh_edge: bfloat16 [253952, 512], P(('band', 'region')), may hold values from -6 to 6
- mesh_sender: int32 [253952], P(('band', 'region')), may hold values from 0 to 255
- mesh_receiver: int32 [253952], P(('band', 'region')), may hold values from 0 to 255
- mesh_live: int32 [128, 35], P(('band', 'region')), may hold values from 1 to 576, as said below
- grid_first: bfloat16 [512, 512], replicated, may hold values from -0.25 to 0.25
- grid_second: bfloat16 [512, 512], replicated, may hold values from -0.25 to 0.25
- grid_gain: float32 [512], replicated, may hold values from 0.5 to 1.5
- encode_send: bfloat16 [512, 512], replicated, may hold values from -0.25 to 0.25
- encode_receive: bfloat16 [512, 512], replicated, may hold values from -0.25 to 0.25
- encode_geometry: float32 [4, 512], replicated, may hold values from -3 to 3
- encode_output: bfloat16 [512, 512], replicated, may hold values from -0.25 to 0.25
- encode_gain: float32 [512], replicated, may hold values from 0.5 to 1.5
- node_first: bfloat16 [1024, 512], replicated, may hold values from -0.1875 to 0.1875
- node_second: bfloat16 [512, 512], replicated, may hold values from -0.25 to 0.25
- node_gain: float32 [512], replicated, may hold values from 0.5 to 1.5
- process_edge: bfloat16 [512, 512], replicated, may hold values from -0.25 to 0.25
- process_send: bfloat16 [512, 512], replicated, may hold values from -0.25 to 0.25
- process_receive: bfloat16 [512, 512], replicated, may hold values from -0.25 to 0.25
- process_output: bfloat16 [512, 512], replicated, may hold values from -0.25 to 0.25
- process_gain: float32 [512], replicated, may hold values from 0.5 to 1.5
- update_first: bfloat16 [1024, 512], replicated, may hold values from -0.1875 to 0.1875
- update_second: bfloat16 [512, 512], replicated, may hold values from -0.25 to 0.25
- update_gain: float32 [512], replicated, may hold values from 0.5 to 1.5
Outputs:
- grid_out: bfloat16 [131072, 512], P(('band', 'region'))
- mesh_out: bfloat16 [8192, 512], P('region')
- edge_out: bfloat16 [253952, 512], P(('band', 'region'))
The draws below stay inside these ranges and needn't reach their ends.
Inputs may be any that keep to these rules, and one draw needn't show every extreme that they name: `encode_live`: live encoder edges of each block: columns 0 to 2 count slots of blocks of 2048, the others of blocks of 8; slots past the count are padding. Every draw has a device whose blocks are all full. `mesh_live`: live processor edges of each block: columns 0 to 2 count slots of blocks of 576, the others of blocks of 8; slots past the count are padding. Every draw has a device whose blocks are all full.
All inputs are finite; a program needn't handle non-finite values.
Results may differ from the reference program's by a relative error of at most 0.014.
Values may be sent and summed in bfloat16 or wider, within the bound.
No kernel may reach another device: no remote copies, remote signals or barrier semaphores. Data moves between devices by JAX's collectives and lax.ppermute only.
A program may use at most 128 MiB of HBM per device.

```python
import jax
import jax.numpy as jnp
from jax import lax

D = 512
H = 512
GEOM = 4
GRID_DEV = 1024
MESH_DEV = 256
NEAR_G = 2048
FAR_G = 8
NEAR_M = 576
FAR_M = 8
G2M_DEV = 6400
M2M_DEV = 1984
GRID_ALL = 131072
MESH_ALL = 8192
G2M_ALL = 819200
M2M_ALL = 253952
N_REGION = 32
DEVICES = 128


def block_counts(key, near_cap, far_cap):
    first_key, second_key = jax.random.split(key)
    width = N_REGION + 3
    columns = jnp.arange(width, dtype=jnp.int32)[None, :]
    caps = jnp.broadcast_to(jnp.where(columns < 3, near_cap, far_cap).astype(jnp.int32), (DEVICES, width))
    uniform_draw = jax.random.randint(first_key, (DEVICES, width), 1, caps + 1)
    row_ids = jnp.arange(DEVICES, dtype=jnp.int32)[:, None]
    band_id = row_ids // N_REGION
    polar_band = (band_id == 0) | (band_id == DEVICES // N_REGION - 1)
    counts = jnp.where(polar_band, (uniform_draw + caps + 1) // 2, (uniform_draw + 1) // 2)
    full_row = jax.random.randint(second_key, (), 0, DEVICES)
    return jnp.where(row_ids == full_row, caps, counts).astype(jnp.int32)


def draw_encode_live(key, part):
    key = jax.random.fold_in(key, 11)
    return block_counts(key, NEAR_G, FAR_G)


def draw_mesh_live(key, part):
    key = jax.random.fold_in(key, 23)
    return block_counts(key, NEAR_M, FAR_M)


def place_ends(drawn, stream_key, low, high):
    longest = drawn.shape.index(max(drawn.shape))
    spots = []
    for shift in (0, 1):
        where = [jax.random.randint(jax.random.fold_in(stream_key, axis), (), 0, length) for axis, length in enumerate(drawn.shape)]
        where[longest] = (where[longest] + shift) % drawn.shape[longest]
        spots.append(tuple(where))
    return drawn.at[spots[0]].set(low).at[spots[1]].set(high)


def block_scale(own_key, extent, cuts, least, largest):
    gain = 1.0
    for dim, parts in cuts:
        steps = jax.random.uniform(jax.random.fold_in(jax.random.fold_in(own_key, 6), dim), (parts,), jnp.float32, least / len(cuts), largest / len(cuts))
        gain = gain * jnp.repeat(jnp.exp(steps), extent[dim] // parts).reshape((-1,) + (1,) * (len(extent) - 1 - dim))
    return gain


def centred(stream_key, dims, scale, most, shards=(), kind=jnp.bfloat16):
    array = jax.random.normal(stream_key, dims, jnp.float32) * scale
    if len(shards) > 0:
        array = block_scale(stream_key, dims, shards, -0.22, 0.18) * array
    return jnp.clip(array, min=-most, max=most).astype(kind)


def setup_inputs(seed: int = 0) -> dict:
    key_of = jax.random.split(jax.random.key(seed), 30)
    return {
        "grid_latent": centred(key_of[0], (GRID_ALL, D), 1.0, 6.0, ((0, 128),)),
        "mesh_latent": centred(key_of[1], (MESH_ALL, D), 1.0, 6.0, ((0, 32),)),
        "encode_sender": place_ends(jax.random.randint(key_of[2], (G2M_ALL,), 0, GRID_DEV), jax.random.fold_in(key_of[2], 1), 0, GRID_DEV - 1).astype(jnp.int32),
        "encode_receiver": place_ends(jax.random.randint(key_of[3], (G2M_ALL,), 0, MESH_DEV), jax.random.fold_in(key_of[3], 1), 0, MESH_DEV - 1).astype(jnp.int32),
        "encode_live": draw_encode_live(jax.random.fold_in(key_of[29], 71), 0),
        "encode_feature": centred(key_of[5], (GEOM, G2M_ALL), 1.0, 6.0, ((1, 128),), jnp.float32),
        "mesh_edge": centred(key_of[6], (M2M_ALL, D), 1.0, 6.0, ((0, 128),)),
        "mesh_sender": place_ends(jax.random.randint(key_of[7], (M2M_ALL,), 0, MESH_DEV), jax.random.fold_in(key_of[7], 1), 0, MESH_DEV - 1).astype(jnp.int32),
        "mesh_receiver": place_ends(jax.random.randint(key_of[8], (M2M_ALL,), 0, MESH_DEV), jax.random.fold_in(key_of[8], 1), 0, MESH_DEV - 1).astype(jnp.int32),
        "mesh_live": draw_mesh_live(jax.random.fold_in(key_of[29], 71), 0),
        "grid_first": centred(key_of[10], (D, H), D ** -0.5, 0.25),
        "grid_second": centred(key_of[11], (H, D), H ** -0.5, 0.25),
        "grid_gain": jnp.clip(1.0 + 0.1 * jax.random.normal(key_of[12], (D,), jnp.float32), 0.5, 1.5),
        "encode_send": centred(key_of[13], (D, H), D ** -0.5, 0.25),
        "encode_receive": centred(key_of[14], (D, H), D ** -0.5, 0.25),
        "encode_geometry": centred(key_of[15], (GEOM, H), GEOM ** -0.5, 3.0, (), jnp.float32),
        "encode_output": centred(key_of[16], (H, D), H ** -0.5, 0.25),
        "encode_gain": jnp.clip(1.0 + 0.1 * jax.random.normal(key_of[17], (D,), jnp.float32), 0.5, 1.5),
        "node_first": centred(key_of[18], (2 * D, H), (2 * D) ** -0.5, 0.1875),
        "node_second": centred(key_of[19], (H, D), H ** -0.5, 0.25),
        "node_gain": jnp.clip(1.0 + 0.1 * jax.random.normal(key_of[20], (D,), jnp.float32), 0.5, 1.5),
        "process_edge": centred(key_of[21], (D, H), D ** -0.5, 0.25),
        "process_send": centred(key_of[22], (D, H), D ** -0.5, 0.25),
        "process_receive": centred(key_of[23], (D, H), D ** -0.5, 0.25),
        "process_output": centred(key_of[24], (H, D), H ** -0.5, 0.25),
        "process_gain": jnp.clip(1.0 + 0.1 * jax.random.normal(key_of[25], (D,), jnp.float32), 0.5, 1.5),
        "update_first": centred(key_of[26], (2 * D, H), (2 * D) ** -0.5, 0.1875),
        "update_second": centred(key_of[27], (H, D), H ** -0.5, 0.25),
        "update_gain": jnp.clip(1.0 + 0.1 * jax.random.normal(key_of[28], (D,), jnp.float32), 0.5, 1.5),
    }


EPSILON = 1e-05

def layer_norm(values):
    center = values - lax.optimization_barrier(jnp.mean(values, axis=-1, keepdims=True))
    spread = lax.optimization_barrier(jnp.mean(center * center, axis=-1, keepdims=True))
    return center * lax.rsqrt(spread + EPSILON)

def edge_message(preact, w_output, gain_row, live_mask):
    hidden = jax.nn.silu(preact).astype(jnp.bfloat16)
    message = (layer_norm(jnp.dot(hidden, w_output, preferred_element_type=jnp.float32)) * gain_row).astype(jnp.bfloat16)
    return jnp.where(live_mask[:, None], message, jnp.zeros_like(message))

def node_update(latent, summed, w_first, w_second, gain_row):
    joined = jnp.concatenate([latent, summed.astype(jnp.bfloat16)], axis=1)
    hidden = jax.nn.silu(jnp.dot(joined, w_first, preferred_element_type=jnp.float32)).astype(jnp.bfloat16)
    update = layer_norm(jnp.dot(hidden, w_second, preferred_element_type=jnp.float32)) * gain_row
    return (latent.astype(jnp.float32) + update).astype(jnp.bfloat16)

def slot_layout(live_table, group_id, near_cap, far_cap):
    per_dev = 3 * near_cap + N_REGION * far_cap
    position = jnp.arange(per_dev, dtype=jnp.int32)
    near_part = position < 3 * near_cap
    far_pos = position - 3 * near_cap
    column_id = jnp.where(near_part, position // near_cap, 3 + jnp.maximum(far_pos, 0) // far_cap).astype(jnp.int32)
    slot_id = jnp.where(near_part, position % near_cap, jnp.maximum(far_pos, 0) % far_cap).astype(jnp.int32)
    counts = lax.dynamic_index_in_dim(live_table, group_id, 0, keepdims=False)
    live_mask = slot_id < jnp.take(counts, column_id, axis=0)
    home = group_id % N_REGION
    source = jnp.where(near_part, (home + column_id - 1 + N_REGION) % N_REGION, column_id - 3).astype(jnp.int32)
    return (source, live_mask)

def reference(grid_latent, mesh_latent, encode_sender, encode_receiver, encode_live, encode_feature, mesh_edge, mesh_sender, mesh_receiver, mesh_live, grid_first, grid_second, grid_gain, encode_send, encode_receive, encode_geometry, encode_output, encode_gain, node_first, node_second, node_gain, process_edge, process_send, process_receive, process_output, process_gain, update_first, update_second, update_gain):
    grid_hidden = jax.nn.silu(jnp.dot(grid_latent, grid_first, preferred_element_type=jnp.float32)).astype(jnp.bfloat16)
    grid_update = layer_norm(jnp.dot(grid_hidden, grid_second, preferred_element_type=jnp.float32)) * grid_gain
    grid_out = (grid_latent.astype(jnp.float32) + grid_update).astype(jnp.bfloat16)
    groups = jnp.arange(DEVICES, dtype=jnp.int32)
    receive_term = jnp.dot(mesh_latent, encode_receive, preferred_element_type=jnp.float32)

    def encode_step(running, group_id):
        band_id = group_id // N_REGION
        column = group_id % N_REGION
        first_slot = (group_id * G2M_DEV).astype(jnp.int32)
        senders = lax.dynamic_slice_in_dim(encode_sender, first_slot, G2M_DEV, 0)
        receivers = lax.dynamic_slice_in_dim(encode_receiver, first_slot, G2M_DEV, 0)
        features = lax.dynamic_slice_in_dim(encode_feature, first_slot, G2M_DEV, 1)
        source, live_mask = slot_layout(encode_live, group_id, NEAR_G, FAR_G)
        sent_rows = jnp.take(grid_latent, (band_id * N_REGION + source) * GRID_DEV + senders, axis=0)
        targets = column * MESH_DEV + receivers
        preact = jnp.dot(sent_rows, encode_send, preferred_element_type=jnp.float32)
        preact = preact + jnp.take(receive_term, targets, axis=0)
        preact = preact + jnp.einsum('ke,kh->eh', features, encode_geometry, precision=lax.Precision.HIGHEST)
        message = edge_message(preact, encode_output, encode_gain, live_mask)
        return (running + jax.ops.segment_sum(message.astype(jnp.float32), targets, num_segments=MESH_ALL), None)
    encode_sum, _ = lax.scan(encode_step, jnp.zeros((MESH_ALL, D), jnp.float32), groups)
    mesh_mid = node_update(mesh_latent, encode_sum, node_first, node_second, node_gain)
    process_term = jnp.dot(mesh_mid, process_receive, preferred_element_type=jnp.float32)

    def process_step(running, group_id):
        column = group_id % N_REGION
        first_slot = (group_id * M2M_DEV).astype(jnp.int32)
        senders = lax.dynamic_slice_in_dim(mesh_sender, first_slot, M2M_DEV, 0)
        receivers = lax.dynamic_slice_in_dim(mesh_receiver, first_slot, M2M_DEV, 0)
        latents = lax.dynamic_slice_in_dim(mesh_edge, first_slot, M2M_DEV, 0)
        source, live_mask = slot_layout(mesh_live, group_id, NEAR_M, FAR_M)
        sent_rows = jnp.take(mesh_mid, source * MESH_DEV + senders, axis=0)
        targets = column * MESH_DEV + receivers
        preact = jnp.dot(latents, process_edge, preferred_element_type=jnp.float32)
        preact = preact + jnp.dot(sent_rows, process_send, preferred_element_type=jnp.float32)
        preact = preact + jnp.take(process_term, targets, axis=0)
        message = edge_message(preact, process_output, process_gain, live_mask)
        updated = (latents.astype(jnp.float32) + message.astype(jnp.float32)).astype(jnp.bfloat16)
        running = running + jax.ops.segment_sum(message.astype(jnp.float32), targets, num_segments=MESH_ALL)
        return (running, updated)
    process_sum, edge_blocks = lax.scan(process_step, jnp.zeros((MESH_ALL, D), jnp.float32), groups)
    mesh_out = node_update(mesh_mid, process_sum, update_first, update_second, update_gain)
    edge_out = edge_blocks.reshape(M2M_ALL, D)
    return (grid_out, mesh_out, edge_out)
```

```python
import functools

import jax
import jax.numpy as jnp
from jax import lax
from jax.experimental import pallas as pl
from jax.experimental.pallas import tpu as pltpu
from jax.sharding import PartitionSpec as P

NEAR_G = 2048
FAR_G = 8
NEAR_M = 576
FAR_M = 8
EPSILON = 1e-05
D = 512
NODES = 256
GRID = 1024
N_REG = 32
FAR = N_REG * FAR_G
NG = 3 * NEAR_G
NM = 3 * NEAR_M
NM_PAD = 1792
M2M = NM + FAR
BF = jnp.bfloat16
F32 = jnp.float32
VMEM = pl.BlockSpec(memory_space=pltpu.VMEM)
SMEM = pl.BlockSpec(memory_space=pltpu.SMEM)
ANY = pl.BlockSpec(memory_space=pl.ANY)


def nt(a, b):
    return lax.dot_general(a, b, (((1,), (1,)), ((), ())), preferred_element_type=F32)


def nn(a, b):
    return jnp.dot(a, b, preferred_element_type=F32)


def identity(n):
    row = lax.broadcasted_iota(jnp.int32, (n, n), 0)
    return (row == lax.broadcasted_iota(jnp.int32, (n, n), 1)).astype(F32).astype(BF)


def one_hot(rows, index):
    row = lax.broadcasted_iota(jnp.int32, (rows, index.shape[1]), 0).astype(jnp.int16)
    return jnp.where(row == index.astype(jnp.int16), jnp.ones((), BF), jnp.zeros((), BF))


def centred_t(weight):
    w_t = nt(identity(D), weight)
    return (w_t - jnp.mean(w_t, axis=0, keepdims=True)).astype(BF)


def feature_rows(feature):
    high = feature.astype(BF).astype(F32)
    zero = jnp.zeros(feature.shape, F32)
    return jnp.concatenate([high, feature - high, high, zero], axis=0).astype(BF)


def messages_t(half_pre, w_out_t, live):
    hidden = (half_pre * jnp.tanh(half_pre) + half_pre).astype(BF)
    y = nn(w_out_t, hidden)
    spread = jnp.sum(y * y, axis=0, keepdims=True) * (1 / D)
    scale = jnp.where(live, lax.rsqrt(spread + EPSILON), 0.0)
    return (y * scale).astype(BF)


def far_live(counts, width, near_cols):
    lane = lax.broadcasted_iota(jnp.int32, (1, width), 1)
    limit = jnp.zeros((1, width), jnp.int32)
    for k in range(N_REG):
        limit = jnp.where(lane // FAR_G == k, counts[0, 3 + k], limit)
    return lane % FAR_G < limit


def call(kernel, outs, in_specs, args, scratch=(), out_specs=None, flops=0, name=None, aliases=None):
    return pl.pallas_call(
        kernel,
        out_shape=outs,
        in_specs=in_specs,
        out_specs=jax.tree.map(lambda _: VMEM, outs) if out_specs is None else out_specs,
        scratch_shapes=list(scratch),
        compiler_params=pltpu.CompilerParams(vmem_limit_bytes=48 * 2**20),
        cost_estimate=pl.CostEstimate(flops=flops, bytes_accessed=2**20, transcendentals=0),
        input_output_aliases=aliases or {},
        name=name,
    )(*args)


def shape(dims, kind):
    return jax.ShapeDtypeStruct(dims, kind)


def encode_block(table, rt, gt, wt, sender, receiver, feature, live):
    hot = one_hot(NODES, receiver)
    pre = nn(table, one_hot(GRID, sender)) + nn(rt, hot) + nn(gt, feature_rows(feature))
    return nt(hot, messages_t(pre, wt, live))


def own_kernel(live, grid, mesh, sender, receiver, feature, w_send, w_recv, geo, w_out, out, wst, rt, gt, wt):
    eye = identity(D)
    wst[...] = (0.5 * nt(eye, w_send[...])).astype(BF)
    table = nt(wst[...], grid[...]).astype(BF)
    wrt = nt(eye, w_recv[...]).astype(BF)
    rt[...] = (0.5 * nt(wrt, mesh[...])).astype(BF)
    wt[...] = centred_t(w_out[...])
    half = 0.5 * geo[...]
    high = half.astype(BF).astype(F32)
    stacked = jnp.concatenate([high, high, half - high, jnp.zeros((4, D), F32)], axis=0)
    gt[...] = nt(eye, stacked.astype(BF)).astype(BF)
    part = pl.ds(NEAR_G, NEAR_G)
    lane = lax.broadcasted_iota(jnp.int32, (1, NEAR_G), 1)
    out[...] = encode_block(
        table, rt[...], gt[...], wt[...], sender[:, part], receiver[:, part], feature[:, part], lane < live[0, 1]
    )


def sides_kernel(live, before, after, sender, receiver, feature, wst, rt, gt, wt, total, out):
    lane = lax.broadcasted_iota(jnp.int32, (1, NEAR_G), 1)
    value = total[...]
    for q, rows in ((0, before), (2, after)):
        part = pl.ds(q * NEAR_G, NEAR_G)
        table = nt(wst[...], rows[...]).astype(BF)
        value = value + encode_block(
            table, rt[...], gt[...], wt[...], sender[:, part], receiver[:, part], feature[:, part], lane < live[0, q]
        )
    out[...] = value


def far_kernel(live, rows, receiver, feature, wst, rt, gt, wt, total, out):
    part = pl.ds(NG, FAR)
    hot = one_hot(NODES, receiver[:, part])
    pre = nt(wst[...], rows[...]) + nn(rt[...], hot) + nn(gt[...], feature_rows(feature[:, part]))
    message = messages_t(pre, wt[...], far_live(live, FAR, 0))
    out[...] = (total[...] + nt(hot, message)).astype(BF)


def asked_hot(asked, first, nodes):
    row = lax.broadcasted_iota(jnp.int32, (FAR, N_REG), 0)
    spread = (row // FAR_G == lax.broadcasted_iota(jnp.int32, (FAR, N_REG), 1)).astype(F32).astype(BF)
    high = (asked // 32).astype(F32).astype(BF)
    low = (asked % 32).astype(F32).astype(BF)
    value = nn(spread, high) * 32.0 + nn(spread, low)
    lane = lax.broadcasted_iota(jnp.int32, (FAR, 2 * FAR_G), 1)
    slot = lax.broadcasted_iota(jnp.int32, (FAR, 2 * FAR_G), 0) % FAR_G
    index = jnp.sum(jnp.where(lane == slot + first, value, 0.0), axis=1, keepdims=True).astype(jnp.int32)
    node = lax.broadcasted_iota(jnp.int32, (FAR, nodes), 1)
    return (node == index).astype(F32).astype(BF)


def send_kernel(asked, grid, out):
    out[...] = nn(asked_hot(asked[...], 0, GRID), grid[...]).astype(BF)


def norm(values):
    center = values - jnp.mean(values, axis=-1, keepdims=True)
    spread = jnp.mean(center * center, axis=-1, keepdims=True)
    return center * lax.rsqrt(spread + EPSILON)


def silu(values):
    half = 0.5 * values
    return (half * jnp.tanh(half) + half).astype(BF)


def mlp(latent, summed, w_first, w_second, gain):
    merged = nn(latent, w_first[:D, :]) + nn(summed, w_first[D:, :])
    update = norm(nn(silu(merged), w_second[...])) * gain[...]
    return (latent.astype(F32) + update).astype(BF)


def band_sum(p0, p1, p2, p3, edge_gain):
    total = (p0[...].astype(F32) + p2[...].astype(F32)) + (p1[...].astype(F32) + p3[...].astype(F32))
    return (total * edge_gain[...]).astype(BF)


def node_kernel(asked, mesh, p0, p1, p2, p3, edge_gain, w_first, w_second, gain, mid, rows):
    value = mlp(mesh[...], band_sum(p0, p1, p2, p3, edge_gain), w_first, w_second, gain)
    mid[...] = value
    rows[...] = nn(asked_hot(asked[...], FAR_G, NODES), value).astype(BF)


def update_kernel(mid, p0, p1, p2, p3, edge_gain, w_first, w_second, gain, out):
    out[...] = mlp(mid[...], band_sum(p0, p1, p2, p3, edge_gain), w_first, w_second, gain)


def grid_kernel(latent, w_first, w_second, gain, out):
    rows = latent[...]
    update = norm(nn(silu(nn(rows, w_first[...])), w_second[...])) * gain[...]
    out[...] = (rows.astype(F32) + update).astype(BF)


def rows_out(message, edge, gain):
    eye = identity(NODES)
    parts = [nt(eye, message[:, i : i + NODES]) for i in range(0, message.shape[1], NODES)]
    value = parts[0] if len(parts) == 1 else jnp.concatenate(parts, axis=0)
    return (edge.astype(F32) + value * gain).astype(BF)


def near_kernel(
    live, before, mid, after, edge, sender, receiver, w_edge, w_send, w_recv, w_out, gain, out, total, wet, wst, pt, wt
):
    eye = identity(D)
    wet[...] = (0.5 * nt(eye, w_edge[...])).astype(BF)
    wst[...] = (0.5 * nt(eye, w_send[...])).astype(BF)
    wrt = (0.5 * nt(eye, w_recv[...])).astype(BF)
    wt[...] = centred_t(w_out[...])
    pt[...] = nt(wrt, mid[...]).astype(BF)
    table = nt(wst[...], jnp.concatenate([before[...], mid[...], after[...]], axis=0)).astype(BF)
    lane = lax.broadcasted_iota(jnp.int32, (1, NM_PAD), 1)
    block = lane // NEAR_M
    count = jnp.where(block == 0, live[0, 0], jnp.where(block == 1, live[0, 1], live[0, 2]))
    mask = (lane - block * NEAR_M < count) & (lane < NM)
    part = pl.ds(0, NM_PAD)
    hot = one_hot(NODES, receiver[:, part])
    edges = edge[:NM_PAD, :]
    index = jnp.where(lane < NM, sender[:, part] + block * NODES, -1)
    pre = nt(wet[...], edges) + nn(table, one_hot(3 * NODES, index)) + nn(pt[...], hot)
    message = messages_t(pre, wt[...], mask)
    total[...] = nt(hot, message)
    out[:NM, :] = rows_out(message, edges, gain[...])[:NM, :]


def last_kernel(live, rows, edge, receiver, wet, wst, pt, wt, gain, total, edge_out, out, partial, held, sem):
    hot = one_hot(NODES, receiver[:, NM:M2M])
    edges = edge[NM:, :]
    pre = nt(wet[...], edges) + nt(wst[...], rows[...]) + nn(pt[...], hot)
    message = messages_t(pre, wt[...], far_live(live, FAR, 0))
    partial[...] = (total[...] + nt(hot, message)).astype(BF)
    held[...] = rows_out(message, edges, gain[...])
    copy = pltpu.make_async_copy(held, out.at[pl.ds(NM, FAR), :], sem)
    copy.start()
    copy.wait()


def band_parts(partial):
    count = lax.axis_size("band")
    moved = [
        lax.ppermute(partial, "band", [(i, (i + k) % count) for i in range(count)]) for k in range(1, count)
    ]
    return [partial] + moved


def halo(x):
    count = lax.axis_size("region")
    up = [(i, (i + 1) % count) for i in range(count)]
    down = [(j, i) for i, j in up]
    return lax.ppermute(x, "region", up), lax.ppermute(x, "region", down)


def exchange(x):
    return lax.all_to_all(x, "region", split_axis=0, concat_axis=0, tiled=True)


def on_device(
    grid_latent,
    mesh_latent,
    encode_sender,
    encode_receiver,
    encode_live,
    encode_feature,
    mesh_edge,
    mesh_sender,
    mesh_receiver,
    mesh_live,
    grid_first,
    grid_second,
    grid_gain,
    encode_send,
    encode_receive,
    encode_geometry,
    encode_output,
    encode_gain,
    node_first,
    node_second,
    node_gain,
    process_edge,
    process_send,
    process_receive,
    process_output,
    process_gain,
    update_first,
    update_second,
    update_gain,
):
    asks = jnp.concatenate(
        [encode_sender[NG:].reshape(N_REG, FAR_G), mesh_sender[NM:].reshape(N_REG, FAR_M)], axis=1
    )
    asked = exchange(asks)
    before, after = halo(grid_latent)
    sender = encode_sender.reshape(1, -1)
    receiver = encode_receiver.reshape(1, -1)
    gains = [g.reshape(1, D) for g in (grid_gain, encode_gain, node_gain, process_gain, update_gain)]

    weight = shape((D, D), BF)
    total, wst, rt, gt, wt = call(
        own_kernel,
        (shape((NODES, D), F32), weight, shape((D, NODES), BF), shape((D, 16), BF), weight),
        [SMEM] + [VMEM] * 9,
        (encode_live, grid_latent, mesh_latent, sender, receiver, encode_feature)
        + (encode_send, encode_receive, encode_geometry, encode_output),
        flops=8 * 10**9,
        name="encode_own",
    )
    outgoing = call(
        send_kernel, shape((FAR, D), BF), [VMEM] * 2, (asked, grid_latent), flops=3 * 10**8, name="encode_rows"
    )
    far_rows = exchange(outgoing.reshape(N_REG, FAR_G, D)).reshape(FAR, D)
    total = call(
        sides_kernel,
        shape((NODES, D), F32),
        [SMEM] + [VMEM] * 10,
        (encode_live, before, after, sender, receiver, encode_feature, wst, rt, gt, wt, total),
        flops=11 * 10**9,
        name="encode_sides",
    )
    partial = call(
        far_kernel,
        shape((NODES, D), BF),
        [SMEM] + [VMEM] * 8,
        (encode_live, far_rows, receiver, encode_feature, wst, rt, gt, wt, total),
        flops=10**9,
        name="encode_far",
    )
    partial, grid_rows = lax.optimization_barrier((partial, grid_latent))
    parts = band_parts(partial)
    grid_out = call(
        grid_kernel,
        shape((GRID, D), BF),
        [VMEM] * 4,
        (grid_rows, grid_first, grid_second, gains[0]),
        flops=3 * 10**9,
        name="grid_nodes",
    )
    mid, rows = call(
        node_kernel,
        (shape((NODES, D), BF), shape((FAR, D), BF)),
        [VMEM] * 10,
        (asked, mesh_latent, *parts, gains[1], node_first, node_second, gains[2]),
        flops=10**9,
        name="mesh_nodes",
    )
    far_mesh = exchange(rows.reshape(N_REG, FAR_M, D)).reshape(FAR, D)
    before_mid, after_mid = halo(mid)
    m_sender = mesh_sender.reshape(1, -1)
    m_receiver = mesh_receiver.reshape(1, -1)
    edge_near, m_total, wet, wst, pt, wt = call(
        near_kernel,
        (shape((M2M, D), BF), shape((NODES, D), F32), weight, weight, shape((D, NODES), BF), weight),
        [SMEM] + [VMEM] * 11,
        (mesh_live, before_mid, mid, after_mid, mesh_edge, m_sender, m_receiver)
        + (process_edge, process_send, process_receive, process_output, gains[3]),
        flops=6 * 10**9,
        name="process_near",
    )
    edge_out, m_partial = call(
        last_kernel,
        (shape((M2M, D), BF), shape((NODES, D), BF)),
        [SMEM] + [VMEM] * 9 + [ANY],
        (mesh_live, far_mesh, mesh_edge, m_receiver, wet, wst, pt, wt, gains[3], m_total, edge_near),
        scratch=[pltpu.VMEM((FAR, D), BF), pltpu.SemaphoreType.DMA],
        out_specs=(ANY, VMEM),
        flops=10**9,
        name="process_far",
        aliases={10: 0},
    )
    mesh_out = call(
        update_kernel,
        shape((NODES, D), BF),
        [VMEM] * 9,
        (mid, *band_parts(m_partial), gains[3], update_first, update_second, gains[4]),
        flops=10**9,
        name="mesh_update",
    )
    return (grid_out, mesh_out, edge_out)


def solution(mesh):
    edge = P(("band", "region"))
    rows = P(("band", "region"), None)
    mesh_rows = P("region", None)
    return jax.shard_map(
        on_device,
        mesh=mesh,
        in_specs=(rows, mesh_rows, edge, edge, rows, P(None, ("band", "region")), rows, edge, edge, rows) + (P(),) * 19,
        out_specs=(rows, mesh_rows, rows),
        check_vma=False,
    )
```

```python
import functools

import jax
import jax.numpy as jnp
from jax import lax
from jax.experimental import pallas as pl
from jax.experimental.pallas import tpu as pltpu
from jax.sharding import PartitionSpec as P

NEAR_G = 2048
FAR_G = 8
NEAR_M = 576
FAR_M = 8
EPSILON = 1e-05
D = 512
NODES = 256
GRID = 1024
N_REG = 32
FAR = N_REG * FAR_G
NG = 3 * NEAR_G
NM = 3 * NEAR_M
NM_PAD = 1792
M2M = NM + FAR
BF = jnp.bfloat16
F32 = jnp.float32
VMEM = pl.BlockSpec(memory_space=pltpu.VMEM)
SMEM = pl.BlockSpec(memory_space=pltpu.SMEM)
ANY = pl.BlockSpec(memory_space=pl.ANY)
HBM = pl.BlockSpec(memory_space=pltpu.HBM)
HALF = NEAR_G // 2


def nt(a, b):
    return lax.dot_general(a, b, (((1,), (1,)), ((), ())), preferred_element_type=F32)


def nn(a, b):
    return jnp.dot(a, b, preferred_element_type=F32)


def identity(n):
    row = lax.broadcasted_iota(jnp.int32, (n, n), 0)
    return (row == lax.broadcasted_iota(jnp.int32, (n, n), 1)).astype(F32).astype(BF)


def one_hot(rows, index):
    row = lax.broadcasted_iota(jnp.int32, (rows, index.shape[1]), 0).astype(jnp.int16)
    return jnp.where(row == index.astype(jnp.int16), jnp.ones((), BF), jnp.zeros((), BF))


def centred_t(weight):
    w_t = nt(identity(D), weight)
    return (w_t - jnp.mean(w_t, axis=0, keepdims=True)).astype(BF)


def feature_rows(feature):
    high = feature.astype(BF).astype(F32)
    zero = jnp.zeros(feature.shape, F32)
    return jnp.concatenate([high, feature - high, high, zero], axis=0).astype(BF)


def messages_t(half_pre, w_out_t, live):
    hidden = (half_pre * jnp.tanh(half_pre) + half_pre).astype(BF)
    y = nn(w_out_t, hidden)
    spread = jnp.sum(y * y, axis=0, keepdims=True) * (1 / D)
    scale = jnp.where(live, lax.rsqrt(spread + EPSILON), 0.0)
    return (y * scale).astype(BF)


def far_live(counts, width, near_cols):
    lane = lax.broadcasted_iota(jnp.int32, (1, width), 1)
    limit = jnp.zeros((1, width), jnp.int32)
    for k in range(N_REG):
        limit = jnp.where(lane // FAR_G == k, counts[0, 3 + k], limit)
    return lane % FAR_G < limit


class Late:
    def __init__(self, held, copy):
        self.held, self.copy = held, copy
        self.shape = held.shape

    def __getitem__(self, index):
        if self.copy is not None:
            self.copy.wait()
            self.copy = None
        return self.held[index]


def call(kernel, outs, specs, args, scratch=(), out_specs=None, flops=0, name=None, aliases=None, grant=24):
    late = [i for i, spec in enumerate(specs) if spec in "HA"]
    place = {"S": SMEM, "V": VMEM, "H": HBM, "A": ANY, "R": ANY}
    n_in, n_out = len(args), len(jax.tree.leaves(outs))

    def body(*refs):
        ins, rest = list(refs[:n_in]), refs[n_in:]
        held, sems = rest[n_out : n_out + len(late)], rest[n_out + len(late)]
        copies = [pltpu.make_async_copy(ins[i], held[j], sems.at[j]) for j, i in enumerate(late)]
        for j, i in enumerate(late):
            copies[j].start()
            ins[i] = Late(held[j], copies[j])
        kernel(*ins, *rest[:n_out], *rest[n_out + len(late) + 1 :])
        for i in late:
            if ins[i].copy is not None:
                ins[i].copy.wait()

    return pl.pallas_call(
        body,
        out_shape=outs,
        in_specs=[place[spec] for spec in specs],
        out_specs=jax.tree.map(lambda _: VMEM, outs) if out_specs is None else out_specs,
        scratch_shapes=[pltpu.VMEM(args[i].shape, args[i].dtype) for i in late]
        + [pltpu.SemaphoreType.DMA((len(late),))]
        + list(scratch),
        compiler_params=pltpu.CompilerParams(vmem_limit_bytes=grant * 2**20),
        cost_estimate=pl.CostEstimate(flops=flops, bytes_accessed=2**20, transcendentals=0),
        input_output_aliases=aliases or {},
        name=name,
    )(*args)


def shape(dims, kind):
    return jax.ShapeDtypeStruct(dims, kind)


def encode_block(q, table, rt, gt, wt, sender, receiver, feature, limit):
    value = None
    for i in range(0, NEAR_G, HALF):
        part = slice(q * NEAR_G + i, q * NEAR_G + i + HALF)
        hot = one_hot(NODES, receiver[part].reshape(1, HALF))
        pre = nn(table, one_hot(GRID, sender[part].reshape(1, HALF))) + nn(rt, hot)
        pre = pre + nn(gt, feature_rows(feature[:, part]))
        live = lax.broadcasted_iota(jnp.int32, (1, HALF), 1) + i < limit
        term = nt(hot, messages_t(pre, wt, live))
        value = term if value is None else value + term
    return value


def own_kernel(live, w_send, grid, w_recv, mesh, geo, w_out, sender, receiver, feature, out, wst, rt, gt, wt):
    eye = identity(D)
    wst[...] = (0.5 * nt(eye, w_send[...])).astype(BF)
    table = nt(wst[...], grid[...]).astype(BF)
    wrt = nt(eye, w_recv[...]).astype(BF)
    rt[...] = (0.5 * nt(wrt, mesh[...])).astype(BF)
    half = 0.5 * geo[...]
    high = half.astype(BF).astype(F32)
    stacked = jnp.concatenate([high, high, half - high, jnp.zeros((4, D), F32)], axis=0)
    gt[...] = nt(eye, stacked.astype(BF)).astype(BF)
    wt[...] = centred_t(w_out[...])
    out[...] = encode_block(1, table, rt[...], gt[...], wt[...], sender, receiver, feature, live[0, 1])


def sides_kernel(live, before, wst, sender, receiver, feature, rt, gt, wt, after, total, out):
    value = 0.0
    for q, rows in ((0, before), (2, after)):
        table = nt(wst[...], rows[...]).astype(BF)
        value = value + encode_block(q, table, rt[...], gt[...], wt[...], sender, receiver, feature, live[0, q])
    out[...] = total[...] + value


def far_kernel(live, receiver, feature, rt, gt, wst, rows, wt, total, out):
    part = slice(NG, NG + FAR)
    hot = one_hot(NODES, receiver[part].reshape(1, FAR))
    pre = nn(rt[...], hot) + nn(gt[...], feature_rows(feature[:, part])) + nt(wst[...], rows[...])
    message = messages_t(pre, wt[...], far_live(live, FAR, 0))
    out[...] = (total[...] + nt(hot, message)).astype(BF)


def asked_hot(asked, first, nodes):
    row = lax.broadcasted_iota(jnp.int32, (FAR, N_REG), 0)
    spread = (row // FAR_G == lax.broadcasted_iota(jnp.int32, (FAR, N_REG), 1)).astype(F32).astype(BF)
    high = (asked // 32).astype(F32).astype(BF)
    low = (asked % 32).astype(F32).astype(BF)
    value = nn(spread, high) * 32.0 + nn(spread, low)
    lane = lax.broadcasted_iota(jnp.int32, (FAR, 2 * FAR_G), 1)
    slot = lax.broadcasted_iota(jnp.int32, (FAR, 2 * FAR_G), 0) % FAR_G
    index = jnp.sum(jnp.where(lane == slot + first, value, 0.0), axis=1, keepdims=True).astype(jnp.int32)
    node = lax.broadcasted_iota(jnp.int32, (FAR, nodes), 1)
    return (node == index).astype(F32).astype(BF)


def send_kernel(asked, grid, out):
    out[...] = nn(asked_hot(asked[...], 0, GRID), grid[...]).astype(BF)


def norm(values):
    center = values - jnp.mean(values, axis=-1, keepdims=True)
    spread = jnp.mean(center * center, axis=-1, keepdims=True)
    return center * lax.rsqrt(spread + EPSILON)


def silu(values):
    half = 0.5 * values
    return (half * jnp.tanh(half) + half).astype(BF)


def mlp(latent, summed, w_first, w_second, gain):
    merged = nn(latent, w_first[:D, :]) + nn(summed, w_first[D:, :])
    update = norm(nn(silu(merged), w_second[...])) * gain[...]
    return (latent.astype(F32) + update).astype(BF)


def band_sum(p0, p1, p2, p3, edge_gain):
    total = (p0[...].astype(F32) + p2[...].astype(F32)) + (p1[...].astype(F32) + p3[...].astype(F32))
    return (total * edge_gain[...]).astype(BF)


def node_kernel(asked, mesh, p0, p1, p2, p3, edge_gain, w_first, w_second, gain, mid, rows):
    value = mlp(mesh[...], band_sum(p0, p1, p2, p3, edge_gain), w_first, w_second, gain)
    mid[...] = value
    rows[...] = nn(asked_hot(asked[...], FAR_G, NODES), value).astype(BF)


def update_kernel(mid, p0, p1, p2, p3, edge_gain, w_first, w_second, gain, out):
    out[...] = mlp(mid[...], band_sum(p0, p1, p2, p3, edge_gain), w_first, w_second, gain)


def grid_kernel(latent, w_first, w_second, gain, out):
    rows = latent[...]
    update = norm(nn(silu(nn(rows, w_first[...])), w_second[...])) * gain[...]
    out[...] = (rows.astype(F32) + update).astype(BF)


def rows_out(message, edge, gain):
    eye = identity(NODES)
    parts = [nt(eye, message[:, i : i + NODES]) for i in range(0, message.shape[1], NODES)]
    value = parts[0] if len(parts) == 1 else jnp.concatenate(parts, axis=0)
    return (edge.astype(F32) + value * gain).astype(BF)


def prepare_kernel(w_edge, edge, w_send, w_recv, w_out, near, far, wst, wrt, wt):
    eye = identity(D)
    wet = (0.5 * nt(eye, w_edge[...])).astype(BF)
    near[...] = nt(wet, edge[:NM_PAD, :]).astype(BF)
    far[...] = nt(wet, edge[NM:, :]).astype(BF)
    wst[...] = (0.5 * nt(eye, w_send[...])).astype(BF)
    wrt[...] = (0.5 * nt(eye, w_recv[...])).astype(BF)
    wt[...] = centred_t(w_out[...])


def near_kernel(live, wst, wrt, before, mid, after, sender, receiver, edge_pre, wt, edge, gain, out, total, pt):
    pt[...] = nt(wrt[...], mid[...]).astype(BF)
    table = nt(wst[...], jnp.concatenate([before[...], mid[...], after[...]], axis=0)).astype(BF)
    lane = lax.broadcasted_iota(jnp.int32, (1, NM_PAD), 1)
    block = lane // NEAR_M
    count = jnp.where(block == 0, live[0, 0], jnp.where(block == 1, live[0, 1], live[0, 2]))
    mask = (lane - block * NEAR_M < count) & (lane < NM)
    hot = one_hot(NODES, receiver[:NM_PAD].reshape(1, NM_PAD))
    index = jnp.where(lane < NM, sender[:NM_PAD].reshape(1, NM_PAD) + block * NODES, -1)
    pre = edge_pre[...].astype(F32) + nn(table, one_hot(3 * NODES, index)) + nn(pt[...], hot)
    message = messages_t(pre, wt[...], mask)
    total[...] = nt(hot, message)
    out[:NM, :] = rows_out(message, edge[:NM_PAD, :], gain[...])[:NM, :]


def last_kernel(live, receiver, pt, edge_pre, wst, rows, wt, total, edge, gain, edge_out, out, partial, held, sem):
    hot = one_hot(NODES, receiver[NM:].reshape(1, FAR))
    pre = edge_pre[...].astype(F32) + nn(pt[...], hot) + nt(wst[...], rows[...])
    message = messages_t(pre, wt[...], far_live(live, FAR, 0))
    held[...] = rows_out(message, edge[NM:, :], gain[...])
    copy = pltpu.make_async_copy(held, out.at[pl.ds(NM, FAR), :], sem)
    copy.start()
    partial[...] = (total[...] + nt(hot, message)).astype(BF)
    copy.wait()


def band_parts(partial):
    count = lax.axis_size("band")
    moved = [
        lax.ppermute(partial, "band", [(i, (i + k) % count) for i in range(count)]) for k in range(1, count)
    ]
    return [partial] + moved


def halo(x):
    count = lax.axis_size("region")
    up = [(i, (i + 1) % count) for i in range(count)]
    down = [(j, i) for i, j in up]
    return lax.ppermute(x, "region", up), lax.ppermute(x, "region", down)


def exchange(x):
    return lax.all_to_all(x, "region", split_axis=0, concat_axis=0, tiled=True)


def on_device(
    grid_latent,
    mesh_latent,
    encode_sender,
    encode_receiver,
    encode_live,
    encode_feature,
    mesh_edge,
    mesh_sender,
    mesh_receiver,
    mesh_live,
    grid_first,
    grid_second,
    grid_gain,
    encode_send,
    encode_receive,
    encode_geometry,
    encode_output,
    encode_gain,
    node_first,
    node_second,
    node_gain,
    process_edge,
    process_send,
    process_receive,
    process_output,
    process_gain,
    update_first,
    update_second,
    update_gain,
):
    asks = jnp.concatenate(
        [encode_sender[NG:].reshape(N_REG, FAR_G), mesh_sender[NM:].reshape(N_REG, FAR_M)], axis=1
    )
    asked = exchange(asks)
    before, after = halo(grid_latent)
    gains = [g.reshape(1, D) for g in (grid_gain, encode_gain, node_gain, process_gain, update_gain)]

    weight = shape((D, D), BF)
    total, wst, rt, gt, wt = call(
        own_kernel,
        (shape((NODES, D), F32), weight, shape((D, NODES), BF), shape((D, 16), BF), weight),
        "SHHHHHHHHH",
        (encode_live, encode_send, grid_latent, encode_receive, mesh_latent, encode_geometry, encode_output)
        + (encode_sender, encode_receiver, encode_feature),
        flops=8 * 10**9,
        name="encode_own",
    )
    outgoing = call(
        send_kernel, shape((FAR, D), BF), "VH", (asked, grid_latent), flops=3 * 10**8, name="encode_rows"
    )
    far_rows = exchange(outgoing.reshape(N_REG, FAR_G, D)).reshape(FAR, D)
    total = call(
        sides_kernel,
        shape((NODES, D), F32),
        "SAAHHHAAAAA",
        (encode_live, before, wst, encode_sender, encode_receiver, encode_feature, rt, gt, wt, after, total),
        flops=11 * 10**9,
        name="encode_sides",
    )
    partial = call(
        far_kernel,
        shape((NODES, D), BF),
        "SHHAAAAAA",
        (encode_live, encode_receiver, encode_feature, rt, gt, wst, far_rows, wt, total),
        flops=10**9,
        name="encode_far",
    )
    partial, later_edge = lax.optimization_barrier((partial, mesh_edge))
    parts = band_parts(partial)
    near_pre, far_pre, p_wst, p_wrt, p_wt = call(
        prepare_kernel,
        (shape((D, NM_PAD), BF), shape((D, FAR), BF), weight, weight, weight),
        "HHHHH",
        (process_edge, later_edge, process_send, process_receive, process_output),
        flops=3 * 10**9,
        name="process_prepare",
    )
    mid, rows = call(
        node_kernel,
        (shape((NODES, D), BF), shape((FAR, D), BF)),
        "VHAAAAHHHH",
        (asked, mesh_latent, *parts, gains[1], node_first, node_second, gains[2]),
        flops=10**9,
        name="mesh_nodes",
    )
    far_mesh = exchange(rows.reshape(N_REG, FAR_M, D)).reshape(FAR, D)
    before_mid, after_mid = halo(mid)
    edge_near, m_total, pt = call(
        near_kernel,
        (shape((M2M, D), BF), shape((NODES, D), F32), shape((D, NODES), BF)),
        "SAAAAAHHAAHH",
        (mesh_live, p_wst, p_wrt, before_mid, mid, after_mid, mesh_sender, mesh_receiver, near_pre, p_wt)
        + (mesh_edge, gains[3]),
        flops=4 * 10**9,
        name="process_near",
    )
    edge_out, m_partial = call(
        last_kernel,
        (shape((M2M, D), BF), shape((NODES, D), BF)),
        "SHAAAAAAHHR",
        (mesh_live, mesh_receiver, pt, far_pre, p_wst, far_mesh, p_wt, m_total, mesh_edge, gains[3], edge_near),
        scratch=[pltpu.VMEM((FAR, D), BF), pltpu.SemaphoreType.DMA],
        out_specs=(ANY, VMEM),
        flops=10**9,
        name="process_far",
        aliases={10: 0},
    )
    m_partial, grid_rows = lax.optimization_barrier((m_partial, grid_latent))
    m_parts = band_parts(m_partial)
    grid_out = call(
        grid_kernel,
        shape((GRID, D), BF),
        "HHHH",
        (grid_rows, grid_first, grid_second, gains[0]),
        flops=3 * 10**9,
        name="grid_nodes",
    )
    mesh_out = call(
        update_kernel,
        shape((NODES, D), BF),
        "AAAAAHHHH",
        (mid, *m_parts, gains[3], update_first, update_second, gains[4]),
        flops=10**9,
        name="mesh_update",
    )
    return (grid_out, mesh_out, edge_out)


def solution(mesh):
    edge = P(("band", "region"))
    rows = P(("band", "region"), None)
    mesh_rows = P("region", None)
    return jax.shard_map(
        on_device,
        mesh=mesh,
        in_specs=(rows, mesh_rows, edge, edge, rows, P(None, ("band", "region")), rows, edge, edge, rows) + (P(),) * 19,
        out_specs=(rows, mesh_rows, rows),
        check_vma=False,
    )
```

```python
import functools

import jax
import jax.numpy as jnp
from jax import lax
from jax.experimental import pallas as pl
from jax.experimental.pallas import tpu as pltpu
from jax.sharding import PartitionSpec as P

NEAR_G = 2048
FAR_G = 8
NEAR_M = 576
FAR_M = 8
EPSILON = 1e-05
D = 512
NODES = 256
GRID = 1024
N_REG = 32
FAR = N_REG * FAR_G
NG = 3 * NEAR_G
NM = 3 * NEAR_M
NM_PAD = 640
M2M = NM + FAR
BF = jnp.bfloat16
F32 = jnp.float32
VMEM = pl.BlockSpec(memory_space=pltpu.VMEM)
SMEM = pl.BlockSpec(memory_space=pltpu.SMEM)
ANY = pl.BlockSpec(memory_space=pl.ANY)
HBM = pl.BlockSpec(memory_space=pltpu.HBM)
HALF = NEAR_G // 2


def nt(a, b):
    return lax.dot_general(a, b, (((1,), (1,)), ((), ())), preferred_element_type=F32)


def nn(a, b):
    return jnp.dot(a, b, preferred_element_type=F32)


def identity(n):
    row = lax.broadcasted_iota(jnp.int32, (n, n), 0)
    return (row == lax.broadcasted_iota(jnp.int32, (n, n), 1)).astype(F32).astype(BF)


def one_hot(rows, index):
    row = lax.broadcasted_iota(jnp.int32, (rows, index.shape[1]), 0).astype(jnp.int16)
    return jnp.where(row == index.astype(jnp.int16), jnp.ones((), BF), jnp.zeros((), BF))


def centred_t(weight):
    w_t = nt(identity(D), weight)
    return (w_t - jnp.mean(w_t, axis=0, keepdims=True)).astype(BF)


def feature_rows(feature):
    high = feature.astype(BF).astype(F32)
    zero = jnp.zeros(feature.shape, F32)
    return jnp.concatenate([high, feature - high, high, zero], axis=0).astype(BF)


def messages_t(half_pre, w_out_t, live):
    hidden = (half_pre * jnp.tanh(half_pre) + half_pre).astype(BF)
    y = nn(w_out_t, hidden)
    spread = jnp.sum(y * y, axis=0, keepdims=True) * (1 / D)
    scale = jnp.where(live, lax.rsqrt(spread + EPSILON), 0.0)
    return (y * scale).astype(BF)


def far_live(counts, width, near_cols):
    lane = lax.broadcasted_iota(jnp.int32, (1, width), 1)
    limit = jnp.zeros((1, width), jnp.int32)
    for k in range(N_REG):
        limit = jnp.where(lane // FAR_G == k, counts[0, 3 + k], limit)
    return lane % FAR_G < limit


class Late:
    def __init__(self, held, copy):
        self.held, self.copy = held, copy
        self.shape = held.shape

    def __getitem__(self, index):
        if self.copy is not None:
            self.copy.wait()
            self.copy = None
        return self.held[index]


def call(kernel, outs, specs, args, scratch=(), out_specs=None, flops=0, name=None, aliases=None, grant=24):
    outs = jax.tree.leaves(outs)
    scratch_in = [i for i, spec in enumerate(specs) if spec in "SHF"]
    keep = [i for i, spec in enumerate(specs) if spec == "K"]
    late = scratch_in + keep
    n_in, n_out, n_keep = len(args), len(outs), len(keep)
    place = {"S": HBM, "H": HBM, "K": HBM, "F": HBM, "V": VMEM, "R": ANY}
    pin = {"S": pltpu.HBM, "H": pltpu.HBM, "K": pltpu.HBM, "F": pltpu.HBM, "V": pltpu.VMEM, "R": pl.ANY}

    def body(*refs):
        ins, rest = list(refs[:n_in]), refs[n_in:]
        targets = list(rest[n_out + n_keep : n_out + n_keep + len(scratch_in)]) + list(rest[n_out : n_out + n_keep])
        rest_scratch = rest[n_out + n_keep + len(scratch_in) :]
        if late:
            sems, rest_scratch = rest_scratch[0], rest_scratch[1:]
        order = sorted(range(len(late)), key=lambda j: late[j])
        for j in order:
            source = ins[late[j]].at[pl.ds(NM, FAR), :] if specs[late[j]] == "F" else ins[late[j]]
            copy = pltpu.make_async_copy(source, targets[j], sems.at[j])
            copy.start()
            ins[late[j]] = Late(targets[j], copy)
        kernel(*ins, *rest[:n_out], *rest_scratch)
        for i in late:
            if ins[i].copy is not None:
                ins[i].copy.wait()

    out_shape = outs + [pltpu.VMEM(args[i].shape, args[i].dtype) for i in keep]
    result = pl.pallas_call(
        body,
        out_shape=out_shape,
        in_specs=[place[spec] for spec in specs],
        out_specs=(list(out_specs) if out_specs else [VMEM] * n_out) + [VMEM] * n_keep,
        scratch_shapes=[
            pltpu.VMEM((FAR, D), BF)
            if specs[i] == "F"
            else (pltpu.SMEM if specs[i] == "S" else pltpu.VMEM)(args[i].shape, args[i].dtype)
            for i in scratch_in
        ]
        + ([pltpu.SemaphoreType.DMA((len(late),))] if late else [])
        + list(scratch),
        compiler_params=pltpu.CompilerParams(vmem_limit_bytes=grant * 2**20),
        cost_estimate=pl.CostEstimate(flops=flops, bytes_accessed=2**20, transcendentals=0),
        input_output_aliases=aliases or {},
        name=name,
    )(*[arg if spec == "R" else pltpu.with_memory_space_constraint(arg, pin[spec]) for arg, spec in zip(args, specs)])
    return result if len(result) > 1 else result[0]


def shape(dims, kind):
    return jax.ShapeDtypeStruct(dims, kind)


def kept(dims, kind):
    return pltpu.VMEM(dims, kind)


def encode_block(q, table, rt, gt, wt, sender, receiver, feature, limit):
    value = None
    for i in range(0, NEAR_G, HALF):
        part = slice(q * NEAR_G + i, q * NEAR_G + i + HALF)
        hot = one_hot(NODES, receiver[part].reshape(1, HALF))
        pre = nn(table, one_hot(GRID, sender[part].reshape(1, HALF))) + nn(rt, hot)
        pre = pre + nn(gt, feature_rows(feature[:, part]))
        live = lax.broadcasted_iota(jnp.int32, (1, HALF), 1) + i < limit
        term = nt(hot, messages_t(pre, wt, live))
        value = term if value is None else value + term
    return value


def slots_to_rows(row, first):
    lane = lax.broadcasted_iota(jnp.int32, (N_REG, FAR), 1)
    mine = lane // FAR_G == lax.broadcasted_iota(jnp.int32, (N_REG, FAR), 0)
    lane = lax.broadcasted_iota(jnp.int32, (2 * FAR_G, FAR), 1)
    pick = (lane % FAR_G + first == lax.broadcasted_iota(jnp.int32, (2 * FAR_G, FAR), 0)).astype(F32).astype(BF)
    high = jnp.where(mine, row // 32, 0).astype(F32).astype(BF)
    low = jnp.where(mine, row % 32, 0).astype(F32).astype(BF)
    return nt(high, pick) * 32.0 + nt(low, pick)


def start_kernel(sender, m_sender, w_send, w_recv, mesh, geo, w_out, grid, receiver, feature, *rest):
    asks, wst, rt, gt, wt = rest[:5]
    far = slots_to_rows(sender[NG:].reshape(1, FAR), 0) + slots_to_rows(m_sender[NM:].reshape(1, FAR), FAR_G)
    asks[...] = far.astype(jnp.int32)
    eye = identity(D)
    wst[...] = (0.5 * nt(eye, w_send[...])).astype(BF)
    wrt = nt(eye, w_recv[...]).astype(BF)
    rt[...] = (0.5 * nt(wrt, mesh[...])).astype(BF)
    half = 0.5 * geo[...]
    high = half.astype(BF).astype(F32)
    stacked = jnp.concatenate([high, high, half - high, jnp.zeros((4, D), F32)], axis=0)
    gt[...] = nt(eye, stacked.astype(BF)).astype(BF)
    wt[...] = centred_t(w_out[...])


def own_kernel(live, grid, wst, sender, receiver, feature, rt, gt, wt, out):
    table = nt(wst[...], grid[...]).astype(BF)
    out[...] = encode_block(1, table, rt[...], gt[...], wt[...], sender, receiver, feature, live[0, 1])


def sides_kernel(live, before, wst, sender, receiver, feature, rt, gt, wt, after, total, out):
    value = 0.0
    for q, rows in ((0, before), (2, after)):
        table = nt(wst[...], rows[...]).astype(BF)
        value = value + encode_block(q, table, rt[...], gt[...], wt[...], sender, receiver, feature, live[0, q])
    out[...] = total[...] + value


def far_kernel(live, receiver, feature, rt, gt, wst, rows, wt, total, out):
    part = slice(NG, NG + FAR)
    hot = one_hot(NODES, receiver[part].reshape(1, FAR))
    pre = nn(rt[...], hot) + nn(gt[...], feature_rows(feature[:, part])) + nt(wst[...], rows[...])
    message = messages_t(pre, wt[...], far_live(live, FAR, 0))
    out[...] = (total[...] + nt(hot, message)).astype(BF)


def asked_hot(asked, first, nodes):
    row = lax.broadcasted_iota(jnp.int32, (FAR, N_REG), 0)
    spread = (row // FAR_G == lax.broadcasted_iota(jnp.int32, (FAR, N_REG), 1)).astype(F32).astype(BF)
    high = (asked // 32).astype(F32).astype(BF)
    low = (asked % 32).astype(F32).astype(BF)
    value = nn(spread, high) * 32.0 + nn(spread, low)
    lane = lax.broadcasted_iota(jnp.int32, (FAR, 2 * FAR_G), 1)
    slot = lax.broadcasted_iota(jnp.int32, (FAR, 2 * FAR_G), 0) % FAR_G
    index = jnp.sum(jnp.where(lane == slot + first, value, 0.0), axis=1, keepdims=True).astype(jnp.int32)
    node = lax.broadcasted_iota(jnp.int32, (FAR, nodes), 1)
    return (node == index).astype(F32).astype(BF)


def send_kernel(asked, grid, out):
    out[...] = nn(asked_hot(asked[...], 0, GRID), grid[...]).astype(BF)


def norm(values):
    center = values - jnp.mean(values, axis=-1, keepdims=True)
    spread = jnp.mean(center * center, axis=-1, keepdims=True)
    return center * lax.rsqrt(spread + EPSILON)


def silu(values):
    half = 0.5 * values
    return (half * jnp.tanh(half) + half).astype(BF)


def mlp(latent, summed, w_first, w_second, gain):
    merged = nn(latent, w_first[:D, :]) + nn(summed, w_first[D:, :])
    update = norm(nn(silu(merged), w_second[...])) * gain[...]
    return (latent.astype(F32) + update).astype(BF)


def band_sum(p0, p1, p2, p3, edge_gain):
    total = (p0[...].astype(F32) + p2[...].astype(F32)) + (p1[...].astype(F32) + p3[...].astype(F32))
    return (total * edge_gain[...]).astype(BF)


def node_kernel(asked, mesh, p0, p1, p2, p3, edge_gain, w_first, w_second, gain, wrt, mid, rows, pt):
    value = mlp(mesh[...], band_sum(p0, p1, p2, p3, edge_gain), w_first, w_second, gain)
    mid[...] = value
    rows[...] = nn(asked_hot(asked[...], FAR_G, NODES), value).astype(BF)
    pt[...] = nt(wrt[...], value).astype(BF)


def update_kernel(mid, p0, p1, p2, p3, edge_gain, w_first, w_second, gain, out):
    out[...] = mlp(mid[...], band_sum(p0, p1, p2, p3, edge_gain), w_first, w_second, gain)


def grid_kernel(latent, w_first, w_second, gain, *rest):
    out = rest[-1]
    rows = latent[...]
    update = norm(nn(silu(nn(rows, w_first[...])), w_second[...])) * gain[...]
    out[...] = (rows.astype(F32) + update).astype(BF)


def rows_out(message, edge, gain, size):
    width = message.shape[1]
    eye = identity(NODES)
    parts = []
    for i in range(0, width, NODES):
        n = min(NODES, width - i)
        parts.append(nt(eye[:n, :n], message[:, i : i + n]))
    value = parts[0] if len(parts) == 1 else jnp.concatenate(parts, axis=0)
    return (edge.astype(F32) + value[:size, :] * gain).astype(BF)


def prepare_kernel(w_edge, edge, w_send, w_recv, w_out, *rest):
    near, far, wst, wrt, wt, held, sem = rest[7:]
    eye = identity(D)
    wet = (0.5 * nt(eye, w_edge[...])).astype(BF)
    for q in range(3):
        held[q] = nt(wet, edge[q * NEAR_M : q * NEAR_M + NM_PAD, :]).astype(BF)
    copy = pltpu.make_async_copy(held, near, sem)
    copy.start()
    far[...] = nt(wet, edge[NM:, :]).astype(BF)
    wst[...] = (0.5 * nt(eye, w_send[...])).astype(BF)
    wrt[...] = (0.5 * nt(eye, w_recv[...])).astype(BF)
    wt[...] = centred_t(w_out[...])
    copy.wait()


def near_kernel(live, wst, mid, before, after, sender, receiver, pt, edge_pre, wt, total, sent, held, sem):
    lane = lax.broadcasted_iota(jnp.int32, (1, NM_PAD), 1)
    value = 0.0
    for q, rows in ((1, mid), (0, before), (2, after)):
        part = slice(q * NEAR_M, q * NEAR_M + NM_PAD)
        table = nt(wst[...], rows[...]).astype(BF)
        hot = one_hot(NODES, receiver[part].reshape(1, NM_PAD))
        pre = nn(table, one_hot(NODES, sender[part].reshape(1, NM_PAD))) + nn(pt[...], hot) + edge_pre[q].astype(F32)
        message = messages_t(pre, wt[...], (lane < live[0, q]) & (lane < NEAR_M))
        held[q] = message
        value = value + nt(hot, message)
    copy = pltpu.make_async_copy(held, sent, sem)
    copy.start()
    total[...] = value
    copy.wait()


def last_kernel(live, receiver, pt, edge_pre, wst, rows, wt, total, partial, sent):
    hot = one_hot(NODES, receiver[NM:].reshape(1, FAR))
    pre = edge_pre[...].astype(F32) + nn(pt[...], hot) + nt(wst[...], rows[...])
    message = messages_t(pre, wt[...], far_live(live, FAR, 0))
    sent[...] = message
    partial[...] = (total[...] + nt(hot, message)).astype(BF)


def edge_kernel(far, near, edge, gain, out, held, sem):
    copies = []
    for q in range(4):
        size = NEAR_M if q < 3 else FAR
        part = slice(q * NEAR_M, q * NEAR_M + size)
        message = near[q] if q < 3 else far[...]
        held[part, :] = rows_out(message, edge[part, :], gain[...], size)
        rows = pl.ds(q * NEAR_M, size)
        copies.append(pltpu.make_async_copy(held.at[rows, :], out.at[rows, :], sem.at[q]))
        copies[-1].start()
    for copy in copies:
        copy.wait()


def band_parts(partial):
    count = lax.axis_size("band")
    moved = [
        lax.ppermute(partial, "band", [(i, (i + k) % count) for i in range(count)]) for k in range(1, count)
    ]
    return [partial] + moved


def halo(x):
    count = lax.axis_size("region")
    up = [(i, (i + 1) % count) for i in range(count)]
    down = [(j, i) for i, j in up]
    return lax.ppermute(x, "region", up), lax.ppermute(x, "region", down)


def exchange(x):
    return lax.all_to_all(x, "region", split_axis=0, concat_axis=0, tiled=True)


def on_device(
    grid_latent,
    mesh_latent,
    encode_sender,
    encode_receiver,
    encode_live,
    encode_feature,
    mesh_edge,
    mesh_sender,
    mesh_receiver,
    mesh_live,
    grid_first,
    grid_second,
    grid_gain,
    encode_send,
    encode_receive,
    encode_geometry,
    encode_output,
    encode_gain,
    node_first,
    node_second,
    node_gain,
    process_edge,
    process_send,
    process_receive,
    process_output,
    process_gain,
    update_first,
    update_second,
    update_gain,
):
    gains = [g.reshape(1, D) for g in (grid_gain, encode_gain, node_gain, process_gain, update_gain)]
    before, after = halo(grid_latent)
    weight = kept((D, D), BF)
    asks, wst, rt, gt, wt, sender, kept_grid, receiver, feature = call(
        start_kernel,
        (kept((N_REG, 2 * FAR_G), jnp.int32), weight, kept((D, NODES), BF), kept((D, 16), BF), weight),
        "KHHHHHHKKK",
        (encode_sender, mesh_sender, encode_send, encode_receive, mesh_latent, encode_geometry, encode_output)
        + (grid_latent, encode_receiver, encode_feature),
        flops=2 * 10**9,
        name="encode_start",
    )
    asked = exchange(asks)
    total = call(
        own_kernel,
        [kept((NODES, D), F32)],
        "SVVVVVVVV",
        (encode_live, kept_grid, wst, sender, receiver, feature, rt, gt, wt),
        flops=6 * 10**9,
        name="encode_own",
    )
    outgoing = call(
        send_kernel, [shape((FAR, D), BF)], "VV", (asked, kept_grid), flops=3 * 10**8, name="encode_rows"
    )
    far_rows = exchange(outgoing.reshape(N_REG, FAR_G, D)).reshape(FAR, D)
    total = call(
        sides_kernel,
        [kept((NODES, D), F32)],
        "SHVVVVVVVHV",
        (encode_live, before, wst, sender, receiver, feature, rt, gt, wt, after, total),
        flops=11 * 10**9,
        name="encode_sides",
    )
    partial = call(
        far_kernel,
        [kept((NODES, D), BF)],
        "SVVVVVVVV",
        (encode_live, receiver, feature, rt, gt, wst, far_rows, wt, total),
        flops=10**9,
        name="encode_far",
    )
    partial, later_edge = lax.optimization_barrier((partial, mesh_edge))
    parts = band_parts(partial)
    prepared = call(
        prepare_kernel,
        (pltpu.HBM((3, D, NM_PAD), BF), kept((D, FAR), BF), weight, weight, weight),
        "HHHHHKKKKKKK",
        (process_edge, later_edge, process_send, process_receive, process_output)
        + (node_first, node_second, mesh_latent, gains[1], gains[2], mesh_sender, mesh_receiver),
        scratch=[pltpu.VMEM((3, D, NM_PAD), BF), pltpu.SemaphoreType.DMA],
        out_specs=(HBM, VMEM, VMEM, VMEM, VMEM),
        flops=3 * 10**9,
        name="process_prepare",
    )
    near_pre, far_pre, p_wst, p_wrt, p_wt, n_first, n_second, n_mesh, n_eg, n_gain, m_sender, m_receiver = prepared
    mid, rows, pt = call(
        node_kernel,
        (kept((NODES, D), BF), shape((FAR, D), BF), kept((D, NODES), BF)),
        "VVVVVVVVVVV",
        (asked, n_mesh, *parts, n_eg, n_first, n_second, n_gain, p_wrt),
        flops=10**9,
        name="mesh_nodes",
    )
    far_mesh = exchange(rows.reshape(N_REG, FAR_M, D)).reshape(FAR, D)
    before_mid, after_mid = halo(mid)
    m_total, near_sent = call(
        near_kernel,
        (kept((NODES, D), F32), pltpu.HBM((3, D, NM_PAD), BF)),
        "SVVVVVVVHV",
        (mesh_live, p_wst, mid, before_mid, after_mid, m_sender, m_receiver, pt, near_pre, p_wt),
        scratch=[pltpu.VMEM((3, D, NM_PAD), BF), pltpu.SemaphoreType.DMA],
        out_specs=(VMEM, HBM),
        flops=4 * 10**9,
        name="process_near",
    )
    m_partial, far_sent = call(
        last_kernel,
        (kept((NODES, D), BF), kept((D, FAR), BF)),
        "SVVVVVVV",
        (mesh_live, m_receiver, pt, far_pre, p_wst, far_mesh, p_wt, m_total),
        flops=10**9,
        name="process_far",
    )
    m_partial, grid_rows = lax.optimization_barrier((m_partial, grid_latent))
    m_parts = band_parts(m_partial)
    edge_out, m_gain = call(
        edge_kernel,
        [pltpu.HBM((M2M, D), BF)],
        "VHHK",
        (far_sent, near_sent, mesh_edge, gains[3]),
        scratch=[pltpu.VMEM((M2M, D), BF), pltpu.SemaphoreType.DMA((4,))],
        out_specs=[HBM],
        flops=3 * 10**9,
        name="process_rows",
    )
    grid_out, u_first, u_second, u_gain = call(
        grid_kernel,
        [shape((GRID, D), BF)],
        "HHHHKKK",
        (grid_rows, grid_first, grid_second, gains[0], update_first, update_second, gains[4]),
        flops=3 * 10**9,
        name="grid_nodes",
    )
    mesh_out = call(
        update_kernel,
        [shape((NODES, D), BF)],
        "VVVVVVVVV",
        (mid, *m_parts, m_gain, u_first, u_second, u_gain),
        flops=10**9,
        name="mesh_update",
    )
    return (grid_out, mesh_out, edge_out)


def solution(mesh):
    edge = P(("band", "region"))
    rows = P(("band", "region"), None)
    mesh_rows = P("region", None)
    return jax.shard_map(
        on_device,
        mesh=mesh,
        in_specs=(rows, mesh_rows, edge, edge, rows, P(None, ("band", "region")), rows, edge, edge, rows) + (P(),) * 19,
        out_specs=(rows, mesh_rows, rows),
        check_vma=False,
    )
```

```python
import functools

import jax
import jax.numpy as jnp
from jax import lax
from jax.experimental import pallas as pl
from jax.experimental.pallas import tpu as pltpu
from jax.sharding import PartitionSpec as P

NEAR_G = 2048
FAR_G = 8
NEAR_M = 576
FAR_M = 8
EPSILON = 1e-05
D = 512
NODES = 256
GRID = 1024
N_REG = 32
FAR = N_REG * FAR_G
NG = 3 * NEAR_G
NM = 3 * NEAR_M
NM_PAD = 640
M2M = NM + FAR
BF = jnp.bfloat16
F32 = jnp.float32
VMEM = pl.BlockSpec(memory_space=pltpu.VMEM)
SMEM = pl.BlockSpec(memory_space=pltpu.SMEM)
ANY = pl.BlockSpec(memory_space=pl.ANY)
HBM = pl.BlockSpec(memory_space=pltpu.HBM)
HALF = NEAR_G // 2


def nt(a, b):
    return lax.dot_general(a, b, (((1,), (1,)), ((), ())), preferred_element_type=F32)


def nn(a, b):
    return jnp.dot(a, b, preferred_element_type=F32)


def identity(n):
    row = lax.broadcasted_iota(jnp.int32, (n, n), 0)
    return (row == lax.broadcasted_iota(jnp.int32, (n, n), 1)).astype(F32).astype(BF)


def one_hot(rows, index):
    row = lax.broadcasted_iota(jnp.int32, (rows, index.shape[1]), 0).astype(jnp.int16)
    return jnp.where(row == index.astype(jnp.int16), jnp.ones((), BF), jnp.zeros((), BF))


def centred_t(weight):
    w_t = nt(identity(D), weight)
    return (w_t - jnp.mean(w_t, axis=0, keepdims=True)).astype(BF)


def feature_rows(feature):
    high = feature.astype(BF).astype(F32)
    zero = jnp.zeros(feature.shape, F32)
    return jnp.concatenate([high, feature - high, high, zero], axis=0).astype(BF)


def messages_t(half_pre, w_out_t, live=None):
    hidden = (half_pre * jnp.tanh(half_pre) + half_pre).astype(BF)
    y = nn(w_out_t, hidden)
    spread = jnp.sum(y * y, axis=0, keepdims=True) * (1 / D)
    scale = lax.rsqrt(spread + EPSILON)
    if live is not None:
        scale = jnp.where(live, scale, 0.0)
    return (y * scale).astype(BF)


def far_live(counts, width):
    lane = lax.broadcasted_iota(jnp.int32, (1, width), 1)
    limit = jnp.zeros((1, width), jnp.int32)
    for k in range(N_REG):
        limit = jnp.where(lane // FAR_G == k, counts[0, 3 + k], limit)
    return lane % FAR_G < limit


class Late:
    def __init__(self, held, copy):
        self.held, self.copy = held, copy
        self.shape = held.shape

    def __getitem__(self, index):
        if self.copy is not None:
            self.copy.wait()
            self.copy = None
        return self.held[index]


def call(kernel, outs, specs, args, scratch=(), out_specs=None, flops=0, name=None, aliases=None, grant=24):
    outs = jax.tree.leaves(outs)
    scratch_in = [i for i, spec in enumerate(specs) if spec in "SHF"]
    keep = [i for i, spec in enumerate(specs) if spec == "K"]
    late = scratch_in + keep
    n_in, n_out, n_keep = len(args), len(outs), len(keep)
    place = {"S": HBM, "H": HBM, "K": HBM, "F": HBM, "V": VMEM, "R": ANY}
    pin = {"S": pltpu.HBM, "H": pltpu.HBM, "K": pltpu.HBM, "F": pltpu.HBM, "V": pltpu.VMEM, "R": pl.ANY}

    def body(*refs):
        ins, rest = list(refs[:n_in]), refs[n_in:]
        targets = list(rest[n_out + n_keep : n_out + n_keep + len(scratch_in)]) + list(rest[n_out : n_out + n_keep])
        rest_scratch = rest[n_out + n_keep + len(scratch_in) :]
        if late:
            sems, rest_scratch = rest_scratch[0], rest_scratch[1:]
        order = sorted(range(len(late)), key=lambda j: late[j])
        for j in order:
            source = ins[late[j]].at[pl.ds(NM, FAR), :] if specs[late[j]] == "F" else ins[late[j]]
            copy = pltpu.make_async_copy(source, targets[j], sems.at[j])
            copy.start()
            ins[late[j]] = Late(targets[j], copy)
        kernel(*ins, *rest[:n_out], *rest_scratch)
        for i in late:
            if ins[i].copy is not None:
                ins[i].copy.wait()

    out_shape = outs + [pltpu.VMEM(args[i].shape, args[i].dtype) for i in keep]
    result = pl.pallas_call(
        body,
        out_shape=out_shape,
        in_specs=[place[spec] for spec in specs],
        out_specs=(list(out_specs) if out_specs else [VMEM] * n_out) + [VMEM] * n_keep,
        scratch_shapes=[
            pltpu.VMEM((FAR, D), BF)
            if specs[i] == "F"
            else (pltpu.SMEM if specs[i] == "S" else pltpu.VMEM)(args[i].shape, args[i].dtype)
            for i in scratch_in
        ]
        + ([pltpu.SemaphoreType.DMA((len(late),))] if late else [])
        + list(scratch),
        compiler_params=pltpu.CompilerParams(vmem_limit_bytes=grant * 2**20),
        cost_estimate=pl.CostEstimate(flops=flops, bytes_accessed=2**20, transcendentals=0),
        input_output_aliases=aliases or {},
        name=name,
    )(*[arg if spec == "R" else pltpu.with_memory_space_constraint(arg, pin[spec]) for arg, spec in zip(args, specs)])
    return result if len(result) > 1 else result[0]


def shape(dims, kind):
    return jax.ShapeDtypeStruct(dims, kind)


def kept(dims, kind):
    return pltpu.VMEM(dims, kind)


def encode_block(q, halves, table, rt, gt, wt, sender, receiver, feature):
    value = None
    for i in halves:
        part = slice(q * NEAR_G + i, q * NEAR_G + i + HALF)
        hot = one_hot(NODES, receiver[:, part])
        pre = nn(table, one_hot(GRID, sender[part].reshape(1, HALF))) + nn(rt, hot)
        pre = pre + nn(gt, feature_rows(feature[:, part]))
        term = nt(hot, messages_t(pre, wt))
        value = term if value is None else value + term
    return value


def slots_to_rows(row, first):
    lane = lax.broadcasted_iota(jnp.int32, (N_REG, FAR), 1)
    mine = lane // FAR_G == lax.broadcasted_iota(jnp.int32, (N_REG, FAR), 0)
    lane = lax.broadcasted_iota(jnp.int32, (2 * FAR_G, FAR), 1)
    pick = (lane % FAR_G + first == lax.broadcasted_iota(jnp.int32, (2 * FAR_G, FAR), 0)).astype(F32).astype(BF)
    high = jnp.where(mine, row // 32, 0).astype(F32).astype(BF)
    low = jnp.where(mine, row % 32, 0).astype(F32).astype(BF)
    return nt(high, pick) * 32.0 + nt(low, pick)


def asks_kernel(sender, m_sender, asks, *_):
    far = slots_to_rows(sender[NG:].reshape(1, FAR), 0) + slots_to_rows(m_sender[NM:].reshape(1, FAR), FAR_G)
    asks[...] = far.astype(jnp.int32)


def weights_kernel(w_send, live, w_recv, mesh, receiver, geo, w_out, *rest):
    wst, rt, gt, wt, targets = rest[2:]
    eye = identity(D)
    wst[...] = (0.5 * nt(eye, w_send[...])).astype(BF)
    wrt = nt(eye, w_recv[...]).astype(BF)
    rt[...] = (0.5 * nt(wrt, mesh[...])).astype(BF)
    lane = lax.broadcasted_iota(jnp.int32, (1, NEAR_G), 1)
    for q in range(3):
        part = slice(q * NEAR_G, (q + 1) * NEAR_G)
        targets[:, part] = jnp.where(lane < live[0, q], receiver[part].reshape(1, NEAR_G), -1)
    targets[:, NG:] = jnp.where(far_live(live, FAR), receiver[NG:].reshape(1, FAR), -1)
    half = 0.5 * geo[...]
    high = half.astype(BF).astype(F32)
    stacked = jnp.concatenate([high, high, half - high, jnp.zeros((4, D), F32)], axis=0)
    gt[...] = nt(eye, stacked.astype(BF)).astype(BF)
    wt[...] = centred_t(w_out[...])


def first_edges_kernel(grid, wst, sender, receiver, feature, rt, gt, wt, out):
    table = nt(wst[...], grid[...]).astype(BF)
    out[...] = encode_block(1, (0,), table, rt[...], gt[...], wt[...], sender, receiver, feature).astype(BF)


def near_edges_kernel(grid, wst, sender, receiver, feature, rt, gt, wt, begun, before, after, out):
    value = begun[...].astype(F32)
    for q, rows in ((1, grid), (0, before), (2, after)):
        table = nt(wst[...], rows[...]).astype(BF)
        halves = (HALF,) if q == 1 else (0, HALF)
        value = value + encode_block(q, halves, table, rt[...], gt[...], wt[...], sender, receiver, feature)
    out[...] = value


def far_kernel(receiver, feature, rt, gt, wst, rows, wt, total, *rest):
    part = slice(NG, NG + FAR)
    hot = one_hot(NODES, receiver[:, part])
    pre = nn(rt[...], hot) + nn(gt[...], feature_rows(feature[:, part])) + nt(wst[...], rows[...])
    split(total[...] + nt(hot, messages_t(pre, wt[...])), *rest[-2:])


def split(value, low, high):
    value = value.astype(BF)
    low[...] = value[: NODES // 2, :]
    high[...] = value[NODES // 2 :, :]


def asked_hot(asked, first, nodes):
    row = lax.broadcasted_iota(jnp.int32, (FAR, N_REG), 0)
    spread = (row // FAR_G == lax.broadcasted_iota(jnp.int32, (FAR, N_REG), 1)).astype(F32).astype(BF)
    high = (asked // 32).astype(F32).astype(BF)
    low = (asked % 32).astype(F32).astype(BF)
    value = nn(spread, high) * 32.0 + nn(spread, low)
    lane = lax.broadcasted_iota(jnp.int32, (FAR, 2 * FAR_G), 1)
    slot = lax.broadcasted_iota(jnp.int32, (FAR, 2 * FAR_G), 0) % FAR_G
    index = jnp.sum(jnp.where(lane == slot + first, value, 0.0), axis=1, keepdims=True).astype(jnp.int32)
    node = lax.broadcasted_iota(jnp.int32, (FAR, nodes), 1)
    return (node == index).astype(F32).astype(BF)


def send_kernel(asked, grid, out):
    out[...] = nn(asked_hot(asked[...], 0, GRID), grid[...]).astype(BF)


def norm(values):
    center = values - jnp.mean(values, axis=-1, keepdims=True)
    spread = jnp.mean(center * center, axis=-1, keepdims=True)
    return center * lax.rsqrt(spread + EPSILON)


def silu(values):
    half = 0.5 * values
    return (half * jnp.tanh(half) + half).astype(BF)


def mlp(latent, summed, w_first, w_second, gain):
    merged = nn(latent, w_first[:D, :]) + nn(summed, w_first[D:, :])
    update = norm(nn(silu(merged), w_second[...])) * gain[...]
    return (latent.astype(F32) + update).astype(BF)


def plus(a, b):
    return a[...].astype(F32) + b[...].astype(F32)


def add_kernel(a, b, out):
    out[...] = plus(a, b).astype(BF)


def band_total(low, low_in, high, high_in, edge_gain):
    return (jnp.concatenate([plus(low, low_in), plus(high, high_in)], axis=0) * edge_gain[...]).astype(BF)


def node_kernel(asked, mesh, p0, p1, p2, p3, edge_gain, w_first, w_second, gain, wrt, mid, rows, pt):
    value = mlp(mesh[...], band_total(p0, p1, p2, p3, edge_gain), w_first, w_second, gain)
    mid[...] = value
    rows[...] = nn(asked_hot(asked[...], FAR_G, NODES), value).astype(BF)
    pt[...] = nt(wrt[...], value).astype(BF)


def update_kernel(mid, p0, p1, p2, p3, edge_gain, w_first, w_second, gain, out):
    out[...] = mlp(mid[...], band_total(p0, p1, p2, p3, edge_gain), w_first, w_second, gain)


def grid_kernel(latent, w_first, w_second, gain, out, held, sems):
    copies = []
    for i in range(4):
        part = slice(i * NODES, (i + 1) * NODES)
        rows = latent[part, :]
        update = norm(nn(silu(nn(rows, w_first[...])), w_second[...])) * gain[...]
        held[part, :] = (rows.astype(F32) + update).astype(BF)
        where = pl.ds(i * NODES, NODES)
        copies.append(pltpu.make_async_copy(held.at[where, :], out.at[where, :], sems.at[i]))
        copies[-1].start()
    for copy in copies:
        copy.wait()


def rows_out(message, edge, gain, size):
    width = message.shape[1]
    eye = identity(NODES)
    parts = []
    for i in range(0, width, NODES):
        n = min(NODES, width - i)
        parts.append(nt(eye[:n, :n], message[:, i : i + n]))
    value = parts[0] if len(parts) == 1 else jnp.concatenate(parts, axis=0)
    return (edge.astype(F32) + value[:size, :] * gain).astype(BF)


def edge_terms_kernel(w_edge, edge, *rest):
    near, far, held, sem = rest[-4:]
    wet = (0.5 * nt(identity(D), w_edge[...])).astype(BF)
    for q in range(3):
        held[:, q * NM_PAD : (q + 1) * NM_PAD] = nt(wet, edge[q * NEAR_M : q * NEAR_M + NM_PAD, :]).astype(BF)
    copy = pltpu.make_async_copy(held, near, sem)
    copy.start()
    far[...] = nt(wet, edge[NM:, :]).astype(BF)
    copy.wait()


def prepare_kernel(w_send, live, sender, receiver, w_recv, w_out, wst, wrt, wt, near, far):
    eye = identity(D)
    wst[...] = (0.5 * nt(eye, w_send[...])).astype(BF)
    wrt[...] = (0.5 * nt(eye, w_recv[...])).astype(BF)
    wt[...] = centred_t(w_out[...])
    lane = lax.broadcasted_iota(jnp.int32, (1, NM_PAD), 1)
    for q in range(3):
        part, put = slice(q * NEAR_M, q * NEAR_M + NM_PAD), slice(q * NM_PAD, (q + 1) * NM_PAD)
        here = (lane < live[0, q]) & (lane < NEAR_M)
        near[0:1, put] = jnp.where(here, receiver[part].reshape(1, NM_PAD), -1)
        near[1:2, put] = sender[part].reshape(1, NM_PAD)
    far[...] = jnp.where(far_live(live, FAR), receiver[NM:].reshape(1, FAR), -1)


def near_kernel(edge_pre, wst, mid, before, after, index, pt, wt, total, sent, held, sem):
    table = nt(wst[...], jnp.concatenate([before[...], mid[...], after[...]], axis=0)).astype(BF)
    target = index[0:1, :]
    hot = one_hot(NODES, target)
    gathered = [
        nn(table[:, q * NODES : (q + 1) * NODES], one_hot(NODES, index[1:2, q * NM_PAD : (q + 1) * NM_PAD]))
        for q in range(3)
    ]
    pre = nn(pt[...], hot) + jnp.concatenate(gathered, axis=1) + edge_pre[...].astype(F32)
    message = messages_t(pre, wt[...], target >= 0)
    held[...] = message
    copy = pltpu.make_async_copy(held, sent, sem)
    copy.start()
    total[...] = nt(hot, message)
    copy.wait()


def last_kernel(target, pt, edge_pre, wst, rows, wt, total, *rest):
    low, high, sent = rest[-3:]
    hot = one_hot(NODES, target[...])
    pre = edge_pre[...].astype(F32) + nn(pt[...], hot) + nt(wst[...], rows[...])
    message = messages_t(pre, wt[...], target[...] >= 0)
    sent[...] = message
    split(total[...] + nt(hot, message), low, high)


def edge_kernel(far, edge, near, gain, *rest):
    out, held, sem = rest[-3:]
    copies = []
    for q in (3, 0, 1, 2):
        size = NEAR_M if q < 3 else FAR
        part = slice(q * NEAR_M, q * NEAR_M + size)
        message = near[:, q * NM_PAD : (q + 1) * NM_PAD] if q < 3 else far[...]
        held[part, :] = rows_out(message, edge[part, :], gain[...], size)
        rows = pl.ds(q * NEAR_M, size)
        copies.append(pltpu.make_async_copy(held.at[rows, :], out.at[rows, :], sem.at[q]))
        copies[-1].start()
    for copy in copies:
        copy.wait()


def swap(x, bit):
    return lax.ppermute(x, "band", [(i, i ^ bit) for i in range(4)])


def band_stages(low, high, first_args, first, second_args, second):
    low, high, first_args = lax.optimization_barrier((low, high, first_args))
    low_in, high_in = swap(low, 1), swap(high, 3)
    first_out = first(first_args)
    low_in, high_in, first_out = lax.optimization_barrier((low_in, high_in, first_out))
    half = kept((NODES // 2, D), BF)
    low = call(add_kernel, [half], "VV", (low, low_in), name="band_add_low")
    low_in = swap(low, 3)
    high = call(add_kernel, [half], "VV", (high, high_in), name="band_add_high")
    high_in = swap(high, 1)
    return (low, low_in, high, high_in), first_out, second(second_args)


def halo(x):
    count = lax.axis_size("region")
    up = [(i, (i + 1) % count) for i in range(count)]
    down = [(j, i) for i, j in up]
    return lax.ppermute(x, "region", up), lax.ppermute(x, "region", down)


def exchange(x):
    return lax.all_to_all(x, "region", split_axis=0, concat_axis=0, tiled=True)


def on_device(
    grid_latent,
    mesh_latent,
    encode_sender,
    encode_receiver,
    encode_live,
    encode_feature,
    mesh_edge,
    mesh_sender,
    mesh_receiver,
    mesh_live,
    grid_first,
    grid_second,
    grid_gain,
    encode_send,
    encode_receive,
    encode_geometry,
    encode_output,
    encode_gain,
    node_first,
    node_second,
    node_gain,
    process_edge,
    process_send,
    process_receive,
    process_output,
    process_gain,
    update_first,
    update_second,
    update_gain,
):
    gains = [g.reshape(1, D) for g in (grid_gain, encode_gain, node_gain, process_gain, update_gain)]
    before, after = halo(grid_latent)
    weight = kept((D, D), BF)
    asks, sender = call(
        asks_kernel,
        [kept((N_REG, 2 * FAR_G), jnp.int32)],
        "KH",
        (encode_sender, mesh_sender),
        name="far_asks",
    )
    asked = exchange(asks)
    asks_sent, w_send = lax.optimization_barrier((asks, encode_send))
    wst, rt, gt, wt, receiver, grid, feature = call(
        weights_kernel,
        (weight, kept((D, NODES), BF), kept((D, 16), BF), weight, kept((1, NG + FAR), jnp.int32)),
        "HSHHHHHKK",
        (w_send, encode_live, encode_receive, mesh_latent, encode_receiver, encode_geometry, encode_output)
        + (grid_latent, encode_feature),
        flops=3 * 10**9,
        name="encode_weights",
    )
    begun = call(
        first_edges_kernel,
        [kept((NODES, D), BF)],
        "VVVVVVVV",
        (grid, wst, sender, receiver, feature, rt, gt, wt),
        flops=3 * 10**9,
        name="encode_begin",
    )
    asked, wst, begun = lax.optimization_barrier((asked, wst, begun))
    outgoing = call(send_kernel, [shape((FAR, D), BF)], "VV", (asked, grid), flops=3 * 10**8, name="encode_rows")
    far_rows = exchange(outgoing.reshape(N_REG, FAR_G, D)).reshape(FAR, D)
    outgoing, wst = lax.optimization_barrier((outgoing, wst))
    total = call(
        near_edges_kernel,
        [kept((NODES, D), F32)],
        "VVVVVVVVVHH",
        (grid, wst, sender, receiver, feature, rt, gt, wt, begun, before, after),
        flops=15 * 10**9,
        name="encode_near",
    )
    half = kept((NODES // 2, D), BF)
    low, high, e_weight, e_rows = call(
        far_kernel,
        (half, half),
        "VVVVVVVVKK",
        (receiver, feature, rt, gt, wst, far_rows, wt, total, process_edge, mesh_edge),
        flops=10**9,
        name="encode_far",
    )

    def edge_terms(args):
        return call(
            edge_terms_kernel,
            (pltpu.HBM((D, 3 * NM_PAD), BF), kept((D, FAR), BF)),
            "VVKKKKKKKKKK",
            args,
            scratch=[pltpu.VMEM((D, 3 * NM_PAD), BF), pltpu.SemaphoreType.DMA],
            out_specs=(HBM, VMEM),
            flops=2 * 10**9,
            name="process_terms",
        )

    def prepare(args):
        return call(
            prepare_kernel,
            (weight, weight, weight, kept((8, 3 * NM_PAD), jnp.int32), kept((1, FAR), jnp.int32)),
            "VSVVVV",
            args,
            flops=2 * 10**9,
            name="process_prepare",
        )

    (low, low_in, high, high_in), terms, _ = band_stages(
        low,
        high,
        (e_weight, e_rows, process_send, mesh_sender, mesh_receiver, process_receive, process_output)
        + (node_first, node_second, mesh_latent, gains[1], gains[2]),
        edge_terms,
        (),
        lambda args: (),
    )
    near_pre, far_pre, p_send, p_from, p_to, p_recv, p_out, n_first, n_second, n_mesh, n_eg, n_gain = terms
    low, high, p_send = lax.optimization_barrier((low, high, p_send))
    p_wst, p_wrt, p_wt, near_index, far_index = prepare((p_send, mesh_live, p_from, p_to, p_recv, p_out))
    parts = (low, low_in, high, high_in)
    mid, rows, pt = call(
        node_kernel,
        (kept((NODES, D), BF), shape((FAR, D), BF), kept((D, NODES), BF)),
        "VVVVVVVVVVV",
        (asked, n_mesh, *parts, n_eg, n_first, n_second, n_gain, p_wrt),
        flops=10**9,
        name="mesh_nodes",
    )
    far_mesh = exchange(rows.reshape(N_REG, FAR_M, D)).reshape(FAR, D)
    before_mid, after_mid = halo(mid)
    m_total, near_sent = call(
        near_kernel,
        (kept((NODES, D), F32), pltpu.HBM((D, 3 * NM_PAD), BF)),
        "HVVVVVVV",
        (near_pre, p_wst, mid, before_mid, after_mid, near_index, pt, p_wt),
        scratch=[pltpu.VMEM((D, 3 * NM_PAD), BF), pltpu.SemaphoreType.DMA],
        out_specs=(VMEM, HBM),
        flops=4 * 10**9,
        name="process_near",
    )
    low, high, far_sent, r_edge = call(
        last_kernel,
        (half, half, kept((D, FAR), BF)),
        "VVVVVVVK",
        (far_index, pt, far_pre, p_wst, far_mesh, p_wt, m_total, mesh_edge),
        flops=10**9,
        name="process_far",
    )

    def edge_rows(args):
        return call(
            edge_kernel,
            [pltpu.HBM((M2M, D), BF)],
            "VVHKKKKKKKK",
            args,
            scratch=[pltpu.VMEM((M2M, D), BF), pltpu.SemaphoreType.DMA((4,))],
            out_specs=[HBM],
            flops=3 * 10**9,
            name="process_rows",
        )

    (low, low_in, high, high_in), from_rows, _ = band_stages(
        low,
        high,
        (far_sent, r_edge, near_sent, gains[3], grid_latent, grid_first, grid_second, gains[0])
        + (update_first, update_second, gains[4]),
        edge_rows,
        (),
        lambda args: (),
    )
    edge_out, m_gain, g_rows, g_first, g_second, g_gain, u_first, u_second, u_gain = from_rows
    low, high, g_rows = lax.optimization_barrier((low, high, g_rows))
    grid_out = call(
        grid_kernel,
        [pltpu.HBM((GRID, D), BF)],
        "VVVV",
        (g_rows, g_first, g_second, g_gain),
        scratch=[pltpu.VMEM((GRID, D), BF), pltpu.SemaphoreType.DMA((4,))],
        out_specs=[HBM],
        flops=3 * 10**9,
        name="grid_nodes",
    )
    grid_out, u_gain = lax.optimization_barrier((grid_out, u_gain))
    parts = (low, low_in, high, high_in)
    mesh_out = call(
        update_kernel,
        [shape((NODES, D), BF)],
        "VVVVVVVVV",
        (mid, *parts, m_gain, u_first, u_second, u_gain),
        flops=10**9,
        name="mesh_update",
    )
    return (grid_out, mesh_out, edge_out)


def solution(mesh):
    edge = P(("band", "region"))
    rows = P(("band", "region"), None)
    mesh_rows = P("region", None)
    return jax.shard_map(
        on_device,
        mesh=mesh,
        in_specs=(rows, mesh_rows, edge, edge, rows, P(None, ("band", "region")), rows, edge, edge, rows) + (P(),) * 19,
        out_specs=(rows, mesh_rows, rows),
        check_vma=False,
    )
```

```python
import functools

import jax
import jax.numpy as jnp
from jax import lax
from jax.experimental import pallas as pl
from jax.experimental.pallas import tpu as pltpu
from jax.sharding import PartitionSpec as P

NEAR_G = 2048
FAR_G = 8
NEAR_M = 576
FAR_M = 8
EPSILON = 1e-05
D = 512
NODES = 256
GRID = 1024
N_REG = 32
FAR = N_REG * FAR_G
NG = 3 * NEAR_G
NM = 3 * NEAR_M
NM_PAD = 640
M2M = NM + FAR
BF = jnp.bfloat16
F32 = jnp.float32
VMEM = pl.BlockSpec(memory_space=pltpu.VMEM)
SMEM = pl.BlockSpec(memory_space=pltpu.SMEM)
ANY = pl.BlockSpec(memory_space=pl.ANY)
HBM = pl.BlockSpec(memory_space=pltpu.HBM)
HALF = NEAR_G // 2


def nt(a, b):
    return lax.dot_general(a, b, (((1,), (1,)), ((), ())), preferred_element_type=F32)


def nn(a, b):
    return jnp.dot(a, b, preferred_element_type=F32)


def identity(n):
    row = lax.broadcasted_iota(jnp.int32, (n, n), 0)
    return (row == lax.broadcasted_iota(jnp.int32, (n, n), 1)).astype(F32).astype(BF)


def one_hot(rows, index):
    row = lax.broadcasted_iota(jnp.int32, (rows, index.shape[1]), 0).astype(jnp.int16)
    return jnp.where(row == index.astype(jnp.int16), jnp.ones((), BF), jnp.zeros((), BF))


def centred_t(weight):
    w_t = nt(identity(D), weight)
    return (w_t - jnp.mean(w_t, axis=0, keepdims=True)).astype(BF)


def feature_rows(feature):
    high = feature.astype(BF).astype(F32)
    zero = jnp.zeros(feature.shape, F32)
    return jnp.concatenate([high, feature - high, high, zero], axis=0).astype(BF)


def messages_t(half_pre, w_out_t, live=None):
    hidden = (half_pre * jnp.tanh(half_pre) + half_pre).astype(BF)
    y = nn(w_out_t, hidden)
    spread = jnp.sum(y * y, axis=0, keepdims=True) * (1 / D)
    scale = lax.rsqrt(spread + EPSILON)
    if live is not None:
        scale = jnp.where(live, scale, 0.0)
    return (y * scale).astype(BF)


def far_live(counts, width):
    lane = lax.broadcasted_iota(jnp.int32, (1, width), 1)
    limit = jnp.zeros((1, width), jnp.int32)
    for k in range(N_REG):
        limit = jnp.where(lane // FAR_G == k, counts[0, 3 + k], limit)
    return lane % FAR_G < limit


class Late:
    def __init__(self, held, copy):
        self.held, self.copy = held, copy
        self.shape = held.shape

    def __getitem__(self, index):
        if self.copy is not None:
            self.copy.wait()
            self.copy = None
        return self.held[index]


def call(kernel, outs, specs, args, scratch=(), out_specs=None, flops=0, name=None, aliases=None, grant=24):
    outs = jax.tree.leaves(outs)
    scratch_in = [i for i, spec in enumerate(specs) if spec in "SHF"]
    keep = [i for i, spec in enumerate(specs) if spec == "K"]
    late = scratch_in + keep
    n_in, n_out, n_keep = len(args), len(outs), len(keep)
    place = {"S": HBM, "H": HBM, "K": HBM, "F": HBM, "V": VMEM, "R": ANY}
    pin = {"S": pltpu.HBM, "H": pltpu.HBM, "K": pltpu.HBM, "F": pltpu.HBM, "V": pltpu.VMEM, "R": pl.ANY}

    def body(*refs):
        ins, rest = list(refs[:n_in]), refs[n_in:]
        targets = list(rest[n_out + n_keep : n_out + n_keep + len(scratch_in)]) + list(rest[n_out : n_out + n_keep])
        rest_scratch = rest[n_out + n_keep + len(scratch_in) :]
        if late:
            sems, rest_scratch = rest_scratch[0], rest_scratch[1:]
        order = sorted(range(len(late)), key=lambda j: late[j])
        for j in order:
            source = ins[late[j]].at[pl.ds(NM, FAR), :] if specs[late[j]] == "F" else ins[late[j]]
            copy = pltpu.make_async_copy(source, targets[j], sems.at[j])
            copy.start()
            ins[late[j]] = Late(targets[j], copy)
        kernel(*ins, *rest[:n_out], *rest_scratch)
        for i in late:
            if ins[i].copy is not None:
                ins[i].copy.wait()

    out_shape = outs + [pltpu.VMEM(args[i].shape, args[i].dtype) for i in keep]
    result = pl.pallas_call(
        body,
        out_shape=out_shape,
        in_specs=[place[spec] for spec in specs],
        out_specs=(list(out_specs) if out_specs else [VMEM] * n_out) + [VMEM] * n_keep,
        scratch_shapes=[
            pltpu.VMEM((FAR, D), BF)
            if specs[i] == "F"
            else (pltpu.SMEM if specs[i] == "S" else pltpu.VMEM)(args[i].shape, args[i].dtype)
            for i in scratch_in
        ]
        + ([pltpu.SemaphoreType.DMA((len(late),))] if late else [])
        + list(scratch),
        compiler_params=pltpu.CompilerParams(vmem_limit_bytes=grant * 2**20),
        cost_estimate=pl.CostEstimate(flops=flops, bytes_accessed=2**20, transcendentals=0),
        input_output_aliases=aliases or {},
        name=name,
    )(*[arg if spec == "R" else pltpu.with_memory_space_constraint(arg, pin[spec]) for arg, spec in zip(args, specs)])
    return result if len(result) > 1 else result[0]


def shape(dims, kind):
    return jax.ShapeDtypeStruct(dims, kind)


def kept(dims, kind):
    return pltpu.VMEM(dims, kind)


def encode_part(begin, size, table, rest, wt, sender, receiver, feature):
    part = slice(begin, begin + size)
    hot = one_hot(NODES, receiver[:, part])
    index = sender[part].reshape(1, size)
    pre = nn(table, one_hot(GRID, index)) + nn(rest[:, :NODES], hot) + nn(rest[:, NODES:], feature_rows(feature[:, part]))
    return nt(hot, messages_t(pre, wt))


def slots_to_rows(row, first):
    lane = lax.broadcasted_iota(jnp.int32, (N_REG, FAR), 1)
    mine = lane // FAR_G == lax.broadcasted_iota(jnp.int32, (N_REG, FAR), 0)
    lane = lax.broadcasted_iota(jnp.int32, (2 * FAR_G, FAR), 1)
    pick = (lane % FAR_G + first == lax.broadcasted_iota(jnp.int32, (2 * FAR_G, FAR), 0)).astype(F32).astype(BF)
    high = jnp.where(mine, row // 32, 0).astype(F32).astype(BF)
    low = jnp.where(mine, row % 32, 0).astype(F32).astype(BF)
    return nt(high, pick) * 32.0 + nt(low, pick)


def asks_kernel(sender, m_sender, asks, *_):
    far = slots_to_rows(sender[NG:].reshape(1, FAR), 0) + slots_to_rows(m_sender[NM:].reshape(1, FAR), FAR_G)
    asks[...] = far.astype(jnp.int32)


def weights_kernel(w_send, live, w_recv, mesh, receiver, geo, w_out, *rest):
    wst, tables, wt, targets = rest[2:]
    eye = identity(D)
    wst[...] = (0.5 * nt(eye, w_send[...])).astype(BF)
    wrt = nt(eye, w_recv[...]).astype(BF)
    tables[:, :NODES] = (0.5 * nt(wrt, mesh[...])).astype(BF)
    lane = lax.broadcasted_iota(jnp.int32, (1, NEAR_G), 1)
    for q in range(3):
        part = slice(q * NEAR_G, (q + 1) * NEAR_G)
        targets[:, part] = jnp.where(lane < live[0, q], receiver[part].reshape(1, NEAR_G), -1)
    targets[:, NG:] = jnp.where(far_live(live, FAR), receiver[NG:].reshape(1, FAR), -1)
    half = 0.5 * geo[...]
    high = half.astype(BF).astype(F32)
    stacked = jnp.concatenate([high, high, half - high, jnp.zeros((4, D), F32)], axis=0)
    tables[:, NODES:] = nt(eye, stacked.astype(BF)).astype(BF)
    wt[...] = centred_t(w_out[...])


def first_edges_kernel(grid, wst, tables, sender, receiver, feature, wt, out, table):
    table[...] = nt(wst[...], grid[...]).astype(BF)
    value = encode_part(NEAR_G, HALF, table[...], tables[...], wt[...], sender, receiver, feature)
    out[...] = value.astype(BF)


def near_edges_kernel(table, wst, tables, sender, receiver, feature, wt, before, after, out):
    rest = (tables[...], wt[...], sender, receiver, feature)
    out[...] = encode_part(NEAR_G + HALF, HALF, table[...], *rest)
    for q, rows in ((0, before), (2, after)):
        side = nt(wst[...], rows[...]).astype(BF)
        value = encode_part(q * NEAR_G, HALF, side, *rest)
        out[...] += value + encode_part(q * NEAR_G + HALF, HALF, side, *rest)


def far_kernel(tables, receiver, feature, rows, wt, total, begun, low, high):
    part = slice(NG, NG + FAR)
    hot = one_hot(NODES, receiver[:, part])
    pre = nn(tables[:, :NODES], hot) + nn(tables[:, NODES:], feature_rows(feature[:, part])) + nt(identity(D), rows[...])
    value = total[...] + nt(hot, messages_t(pre, wt[...]))
    split(value + begun[...].astype(F32), low, high)


def split(value, low, high):
    value = value.astype(BF)
    low[...] = value[: NODES // 2, :]
    high[...] = value[NODES // 2 :, :]


def asked_hot(asked, first, nodes):
    row = lax.broadcasted_iota(jnp.int32, (FAR, N_REG), 0)
    spread = (row // FAR_G == lax.broadcasted_iota(jnp.int32, (FAR, N_REG), 1)).astype(F32).astype(BF)
    high = (asked // 32).astype(F32).astype(BF)
    low = (asked % 32).astype(F32).astype(BF)
    value = nn(spread, high) * 32.0 + nn(spread, low)
    lane = lax.broadcasted_iota(jnp.int32, (FAR, 2 * FAR_G), 1)
    slot = lax.broadcasted_iota(jnp.int32, (FAR, 2 * FAR_G), 0) % FAR_G
    index = jnp.sum(jnp.where(lane == slot + first, value, 0.0), axis=1, keepdims=True).astype(jnp.int32)
    node = lax.broadcasted_iota(jnp.int32, (FAR, nodes), 1)
    return (node == index).astype(F32).astype(BF)


def send_kernel(asked, table, out):
    out[...] = nt(asked_hot(asked[...], 0, GRID), table[...]).astype(BF)


def norm(values):
    center = values - jnp.mean(values, axis=-1, keepdims=True)
    spread = jnp.mean(center * center, axis=-1, keepdims=True)
    return center * lax.rsqrt(spread + EPSILON)


def silu(values):
    half = 0.5 * values
    return (half * jnp.tanh(half) + half).astype(BF)


def mlp(latent, summed, w_first, w_second, gain):
    merged = nn(latent, w_first[:D, :]) + nn(summed, w_first[D:, :])
    update = norm(nn(silu(merged), w_second[...])) * gain[...]
    return (latent.astype(F32) + update).astype(BF)


def plus(a, b):
    return a[...].astype(F32) + b[...].astype(F32)


def add_kernel(a, b, out):
    out[...] = plus(a, b).astype(BF)


def band_total(low, low_in, high, high_in, edge_gain):
    return (jnp.concatenate([plus(low, low_in), plus(high, high_in)], axis=0) * edge_gain[...]).astype(BF)


def node_kernel(asked, mesh, p0, p1, p2, p3, edge_gain, w_first, w_second, gain, wst, wrt, mid, rows, sent, pt):
    value = mlp(mesh[...], band_total(p0, p1, p2, p3, edge_gain), w_first, w_second, gain)
    table = nt(wst[...], value).astype(BF)
    sent[...] = table
    rows[...] = nn(asked_hot(asked[...], FAR_G, NODES), value).astype(BF)
    mid[...] = value
    pt[...] = nt(wrt[...], value).astype(BF)


def update_kernel(mid, p0, p1, p2, p3, edge_gain, w_first, w_second, gain, out):
    out[...] = mlp(mid[...], band_total(p0, p1, p2, p3, edge_gain), w_first, w_second, gain)


def grid_kernel(latent, w_first, w_second, gain, out, held, sems):
    copies = []
    for i in range(2):
        part, where = slice(i * GRID // 2, (i + 1) * GRID // 2), pl.ds(i * GRID // 2, GRID // 2)
        rows = latent[part, :]
        update = norm(nn(silu(nn(rows, w_first[...])), w_second[...])) * gain[...]
        held[part, :] = (rows.astype(F32) + update).astype(BF)
        copies.append(pltpu.make_async_copy(held.at[where, :], out.at[where, :], sems.at[i]))
        copies[-1].start()
    for copy in copies:
        copy.wait()


def rows_out(message, edge, gain, size):
    width = message.shape[1]
    eye = identity(NODES)
    parts = []
    for i in range(0, width, NODES):
        n = min(NODES, width - i)
        parts.append(nt(eye[:n, :n], message[:, i : i + n]))
    value = parts[0] if len(parts) == 1 else jnp.concatenate(parts, axis=0)
    return (edge.astype(F32) + value[:size, :] * gain).astype(BF)


def edge_terms_kernel(w_edge, edge, *rest):
    near, far, held, sems = rest[-4:]
    wet = (0.5 * nt(identity(D), w_edge[...])).astype(BF)
    far[...] = nt(wet, edge[NM:, :]).astype(BF)
    copies = []
    for q in range(3):
        part = slice(q * NM_PAD, (q + 1) * NM_PAD)
        held[:, part] = nt(wet, edge[q * NEAR_M : q * NEAR_M + NM_PAD, :]).astype(BF)
        where = pl.ds(q * NM_PAD, NM_PAD)
        copies.append(pltpu.make_async_copy(held.at[:, where], near.at[:, where], sems.at[q]))
        copies[-1].start()
    for copy in copies:
        copy.wait()


def prepare_kernel(w_send, live, sender, receiver, w_recv, w_out, wst, wrt, wt, near, far):
    eye = identity(D)
    wst[...] = (0.5 * nt(eye, w_send[...])).astype(BF)
    wrt[...] = (0.5 * nt(eye, w_recv[...])).astype(BF)
    wt[...] = centred_t(w_out[...])
    lane = lax.broadcasted_iota(jnp.int32, (1, NM_PAD), 1)
    for q in range(3):
        part, put = slice(q * NEAR_M, q * NEAR_M + NM_PAD), slice(q * NM_PAD, (q + 1) * NM_PAD)
        here = (lane < live[0, q]) & (lane < NEAR_M)
        near[0:1, put] = jnp.where(here, receiver[part].reshape(1, NM_PAD), -1)
        near[1:2, put] = sender[part].reshape(1, NM_PAD)
    far[...] = jnp.where(far_live(live, FAR), receiver[NM:].reshape(1, FAR), -1)


def near_kernel(edge_pre, before, own, after, index, pt, wt, total, sent, held, base, sem):
    target = index[0:1, :]
    hot = one_hot(NODES, target)
    gathered = [
        nn(table[...], one_hot(NODES, index[1:2, q * NM_PAD : (q + 1) * NM_PAD]))
        for q, table in enumerate((before, own, after))
    ]
    base[...] = nn(pt[...], hot) + jnp.concatenate(gathered, axis=1)
    message = messages_t(base[...] + edge_pre[...].astype(F32), wt[...], target >= 0)
    held[...] = message
    copy = pltpu.make_async_copy(held, sent, sem)
    copy.start()
    total[...] = nt(hot, message)
    copy.wait()


def last_kernel(target, pt, edge_pre, wst, rows, wt, total, *rest):
    low, high, sent = rest[-3:]
    hot = one_hot(NODES, target[...])
    pre = edge_pre[...].astype(F32) + nn(pt[...], hot) + nt(wst[...], rows[...])
    message = messages_t(pre, wt[...], target[...] >= 0)
    sent[...] = message
    split(total[...] + nt(hot, message), low, high)


def edge_kernel(far, edge, near, gain, *rest):
    out, held, sem = rest[-3:]
    copies = []
    for q in (3, 0, 1, 2):
        size = NEAR_M if q < 3 else FAR
        part = slice(q * NEAR_M, q * NEAR_M + size)
        message = near[:, q * NM_PAD : (q + 1) * NM_PAD] if q < 3 else far[...]
        held[part, :] = rows_out(message, edge[part, :], gain[...], size)
        rows = pl.ds(q * NEAR_M, size)
        copies.append(pltpu.make_async_copy(held.at[rows, :], out.at[rows, :], sem.at[q]))
        copies[-1].start()
    for copy in copies:
        copy.wait()


def swap(x, bit):
    return lax.ppermute(x, "band", [(i, i ^ bit) for i in range(4)])


def band_stages(low, high, first_args, first, second_args, second):
    low, high, first_args = lax.optimization_barrier((low, high, first_args))
    low_in, high_in = swap(low, 1), swap(high, 3)
    first_out = first(first_args)
    low_in, high_in, first_out = lax.optimization_barrier((low_in, high_in, first_out))
    half = kept((NODES // 2, D), BF)
    low = call(add_kernel, [half], "VV", (low, low_in), name="band_add_low")
    low_in = swap(low, 3)
    high = call(add_kernel, [half], "VV", (high, high_in), name="band_add_high")
    high_in = swap(high, 1)
    return (low, low_in, high, high_in), first_out, second(second_args)


def halo(x):
    count = lax.axis_size("region")
    up = [(i, (i + 1) % count) for i in range(count)]
    down = [(j, i) for i, j in up]
    return lax.ppermute(x, "region", up), lax.ppermute(x, "region", down)


def exchange(x):
    return lax.all_to_all(x, "region", split_axis=0, concat_axis=0, tiled=True)


def on_device(
    grid_latent,
    mesh_latent,
    encode_sender,
    encode_receiver,
    encode_live,
    encode_feature,
    mesh_edge,
    mesh_sender,
    mesh_receiver,
    mesh_live,
    grid_first,
    grid_second,
    grid_gain,
    encode_send,
    encode_receive,
    encode_geometry,
    encode_output,
    encode_gain,
    node_first,
    node_second,
    node_gain,
    process_edge,
    process_send,
    process_receive,
    process_output,
    process_gain,
    update_first,
    update_second,
    update_gain,
):
    gains = [g.reshape(1, D) for g in (grid_gain, encode_gain, node_gain, process_gain, update_gain)]
    before, after = halo(grid_latent)
    weight = kept((D, D), BF)
    asks, sender = call(
        asks_kernel,
        [kept((N_REG, 2 * FAR_G), jnp.int32)],
        "KH",
        (encode_sender, mesh_sender),
        name="far_asks",
    )
    asked = exchange(asks)
    asks_sent, w_send = lax.optimization_barrier((asks, encode_send))
    wst, tables, wt, receiver, grid, feature = call(
        weights_kernel,
        (weight, kept((D, NODES + 16), BF), weight, kept((1, NG + FAR), jnp.int32)),
        "HSHHHHHKK",
        (w_send, encode_live, encode_receive, mesh_latent, encode_receiver, encode_geometry, encode_output)
        + (grid_latent, encode_feature),
        flops=3 * 10**9,
        name="encode_weights",
        grant=56,
    )
    begun, table = call(
        first_edges_kernel,
        (kept((NODES, D), BF), kept((D, GRID), BF)),
        "VVVVVVV",
        (grid, wst, tables, sender, receiver, feature, wt),
        flops=3 * 10**9,
        name="encode_begin",
        grant=56,
    )
    asked, table = lax.optimization_barrier((asked, table))
    outgoing = call(send_kernel, [shape((FAR, D), BF)], "VV", (asked, table), flops=3 * 10**8, name="encode_rows")
    far_rows = exchange(outgoing.reshape(N_REG, FAR_G, D)).reshape(FAR, D)
    outgoing, table = lax.optimization_barrier((outgoing, table))
    total = call(
        near_edges_kernel,
        [kept((NODES, D), F32)],
        "VVVVVVVHH",
        (table, wst, tables, sender, receiver, feature, wt, before, after),
        flops=15 * 10**9,
        name="encode_near",
        grant=56,
    )
    half = kept((NODES // 2, D), BF)
    low, high = call(
        far_kernel,
        (half, half),
        "VVVVVVH",
        (tables, receiver, feature, far_rows, wt, total, begun),
        flops=10**9,
        name="encode_far",
        grant=56,
    )

    def edge_terms(args):
        return call(
            edge_terms_kernel,
            (pltpu.HBM((D, 3 * NM_PAD), BF), kept((D, FAR), BF)),
            "HHKKKKKKKKKK",
            args,
            scratch=[pltpu.VMEM((D, 3 * NM_PAD), BF), pltpu.SemaphoreType.DMA((3,))],
            out_specs=(HBM, VMEM),
            flops=2 * 10**9,
            name="process_terms",
        )

    def prepare(args):
        return call(
            prepare_kernel,
            (weight, weight, weight, kept((8, 3 * NM_PAD), jnp.int32), kept((1, FAR), jnp.int32)),
            "VSVVVV",
            args,
            flops=2 * 10**9,
            name="process_prepare",
        )

    (low, low_in, high, high_in), terms, _ = band_stages(
        low,
        high,
        (process_edge, mesh_edge, process_send, mesh_sender, mesh_receiver, process_receive, process_output)
        + (node_first, node_second, mesh_latent, gains[1], gains[2]),
        edge_terms,
        (),
        lambda args: (),
    )
    near_pre, far_pre, p_send, p_from, p_to, p_recv, p_out, n_first, n_second, n_mesh, n_eg, n_gain = terms
    low, high, p_send = lax.optimization_barrier((low, high, p_send))
    p_wst, p_wrt, p_wt, near_index, far_index = prepare((p_send, mesh_live, p_from, p_to, p_recv, p_out))
    parts = (low, low_in, high, high_in)
    mid, rows, own_table, pt = call(
        node_kernel,
        (kept((NODES, D), BF), shape((FAR, D), BF), kept((D, NODES), BF), kept((D, NODES), BF)),
        "VVVVVVVVVVVV",
        (asked, n_mesh, *parts, n_eg, n_first, n_second, n_gain, p_wst, p_wrt),
        flops=10**9,
        name="mesh_nodes",
    )
    far_mesh = exchange(rows.reshape(N_REG, FAR_M, D)).reshape(FAR, D)
    before_table, after_table = halo(own_table)
    m_total, near_sent = call(
        near_kernel,
        (kept((NODES, D), F32), pltpu.HBM((D, 3 * NM_PAD), BF)),
        "HVVVVVV",
        (near_pre, before_table, own_table, after_table, near_index, pt, p_wt),
        scratch=[pltpu.VMEM((D, 3 * NM_PAD), kind) for kind in (BF, F32)] + [pltpu.SemaphoreType.DMA],
        out_specs=(VMEM, HBM),
        flops=4 * 10**9,
        name="process_near",
    )
    low, high, far_sent = call(
        last_kernel,
        (half, half, kept((D, FAR), BF)),
        "VVVVVVV",
        (far_index, pt, far_pre, p_wst, far_mesh, p_wt, m_total),
        flops=10**9,
        name="process_far",
    )

    def edge_rows(args):
        return call(
            edge_kernel,
            [pltpu.HBM((M2M, D), BF)],
            "VHHKKKKKKKK",
            args,
            scratch=[pltpu.VMEM((M2M, D), BF), pltpu.SemaphoreType.DMA((4,))],
            out_specs=[HBM],
            flops=3 * 10**9,
            name="process_rows",
        )

    (low, low_in, high, high_in), from_rows, _ = band_stages(
        low,
        high,
        (far_sent, mesh_edge, near_sent, gains[3], grid_latent, grid_first, grid_second, gains[0])
        + (update_first, update_second, gains[4]),
        edge_rows,
        (),
        lambda args: (),
    )
    edge_out, m_gain, g_rows, g_first, g_second, g_gain, u_first, u_second, u_gain = from_rows
    low, high, g_rows = lax.optimization_barrier((low, high, g_rows))
    grid_out = call(
        grid_kernel,
        [pltpu.HBM((GRID, D), BF)],
        "VVVV",
        (g_rows, g_first, g_second, g_gain),
        scratch=[pltpu.VMEM((GRID, D), BF), pltpu.SemaphoreType.DMA((2,))],
        out_specs=[HBM],
        flops=3 * 10**9,
        name="grid_nodes",
    )
    grid_out, u_gain = lax.optimization_barrier((grid_out, u_gain))
    parts = (low, low_in, high, high_in)
    mesh_out = call(
        update_kernel,
        [shape((NODES, D), BF)],
        "VVVVVVVVV",
        (mid, *parts, m_gain, u_first, u_second, u_gain),
        flops=10**9,
        name="mesh_update",
    )
    return (grid_out, mesh_out, edge_out)


def solution(mesh):
    edge = P(("band", "region"))
    rows = P(("band", "region"), None)
    mesh_rows = P("region", None)
    return jax.shard_map(
        on_device,
        mesh=mesh,
        in_specs=(rows, mesh_rows, edge, edge, rows, P(None, ("band", "region")), rows, edge, edge, rows) + (P(),) * 19,
        out_specs=(rows, mesh_rows, rows),
        check_vma=False,
    )
```

```python
import functools

import jax
import jax.numpy as jnp
from jax import lax
from jax.experimental import pallas as pl
from jax.experimental.pallas import tpu as pltpu
from jax.sharding import PartitionSpec as P

NEAR_G = 2048
FAR_G = 8
NEAR_M = 576
FAR_M = 8
EPSILON = 1e-05
D = 512
NODES = 256
GRID = 1024
N_REG = 32
FAR = N_REG * FAR_G
NG = 3 * NEAR_G
NM = 3 * NEAR_M
NM_PAD = 640
M2M = NM + FAR
BF = jnp.bfloat16
F32 = jnp.float32
VMEM = pl.BlockSpec(memory_space=pltpu.VMEM)
SMEM = pl.BlockSpec(memory_space=pltpu.SMEM)
ANY = pl.BlockSpec(memory_space=pl.ANY)
HBM = pl.BlockSpec(memory_space=pltpu.HBM)
HALF = NEAR_G // 2


def nt(a, b):
    return lax.dot_general(a, b, (((1,), (1,)), ((), ())), preferred_element_type=F32)


def nn(a, b):
    return jnp.dot(a, b, preferred_element_type=F32)


def identity(n):
    row = lax.broadcasted_iota(jnp.int32, (n, n), 0)
    return (row == lax.broadcasted_iota(jnp.int32, (n, n), 1)).astype(F32).astype(BF)


def one_hot(rows, index):
    row = lax.broadcasted_iota(jnp.int32, (rows, index.shape[1]), 0).astype(jnp.int16)
    return jnp.where(row == index.astype(jnp.int16), jnp.ones((), BF), jnp.zeros((), BF))


def centred_t(weight):
    w_t = nt(identity(D), weight)
    return (w_t - jnp.mean(w_t, axis=0, keepdims=True)).astype(BF)


def feature_rows(feature):
    high = feature.astype(BF).astype(F32)
    zero = jnp.zeros(feature.shape, F32)
    return jnp.concatenate([high, feature - high, high, zero], axis=0).astype(BF)


def messages_t(half_pre, w_out_t, live=None):
    hidden = (half_pre * jnp.tanh(half_pre) + half_pre).astype(BF)
    y = nn(w_out_t, hidden)
    spread = jnp.sum(y * y, axis=0, keepdims=True) * (1 / D)
    scale = lax.rsqrt(spread + EPSILON)
    if live is not None:
        scale = jnp.where(live, scale, 0.0)
    return (y * scale).astype(BF)


def far_live(counts, width):
    lane = lax.broadcasted_iota(jnp.int32, (1, width), 1)
    limit = jnp.zeros((1, width), jnp.int32)
    for k in range(N_REG):
        limit = jnp.where(lane // FAR_G == k, counts[0, 3 + k], limit)
    return lane % FAR_G < limit


class Late:
    def __init__(self, held, copy):
        self.held, self.copy = held, copy
        self.shape = held.shape

    def __getitem__(self, index):
        if self.copy is not None:
            self.copy.wait()
            self.copy = None
        return self.held[index]


def call(kernel, outs, specs, args, scratch=(), out_specs=None, flops=0, name=None, aliases=None, grant=24):
    outs = jax.tree.leaves(outs)
    scratch_in = [i for i, spec in enumerate(specs) if spec in "SHF"]
    keep = [i for i, spec in enumerate(specs) if spec == "K"]
    late = scratch_in + keep
    n_in, n_out, n_keep = len(args), len(outs), len(keep)
    place = {"S": HBM, "H": HBM, "K": HBM, "F": HBM, "V": VMEM, "R": ANY}
    pin = {"S": pltpu.HBM, "H": pltpu.HBM, "K": pltpu.HBM, "F": pltpu.HBM, "V": pltpu.VMEM, "R": pl.ANY}

    def body(*refs):
        ins, rest = list(refs[:n_in]), refs[n_in:]
        targets = list(rest[n_out + n_keep : n_out + n_keep + len(scratch_in)]) + list(rest[n_out : n_out + n_keep])
        rest_scratch = rest[n_out + n_keep + len(scratch_in) :]
        if late:
            sems, rest_scratch = rest_scratch[0], rest_scratch[1:]
        order = sorted(range(len(late)), key=lambda j: late[j])
        for j in order:
            source = ins[late[j]].at[pl.ds(NM, FAR), :] if specs[late[j]] == "F" else ins[late[j]]
            copy = pltpu.make_async_copy(source, targets[j], sems.at[j])
            copy.start()
            ins[late[j]] = Late(targets[j], copy)
        kernel(*ins, *rest[:n_out], *rest_scratch)
        for i in late:
            if ins[i].copy is not None:
                ins[i].copy.wait()

    out_shape = outs + [pltpu.VMEM(args[i].shape, args[i].dtype) for i in keep]
    result = pl.pallas_call(
        body,
        out_shape=out_shape,
        in_specs=[place[spec] for spec in specs],
        out_specs=(list(out_specs) if out_specs else [VMEM] * n_out) + [VMEM] * n_keep,
        scratch_shapes=[
            pltpu.VMEM((FAR, D), BF)
            if specs[i] == "F"
            else (pltpu.SMEM if specs[i] == "S" else pltpu.VMEM)(args[i].shape, args[i].dtype)
            for i in scratch_in
        ]
        + ([pltpu.SemaphoreType.DMA((len(late),))] if late else [])
        + list(scratch),
        compiler_params=pltpu.CompilerParams(vmem_limit_bytes=grant * 2**20),
        cost_estimate=pl.CostEstimate(flops=flops, bytes_accessed=2**20, transcendentals=0),
        input_output_aliases=aliases or {},
        name=name,
    )(*[arg if spec == "R" else pltpu.with_memory_space_constraint(arg, pin[spec]) for arg, spec in zip(args, specs)])
    return result if len(result) > 1 else result[0]


def shape(dims, kind):
    return jax.ShapeDtypeStruct(dims, kind)


def kept(dims, kind):
    return pltpu.VMEM(dims, kind)


def encode_part(begin, size, table, rest, wt, sender, receiver, feature):
    part = slice(begin, begin + size)
    hot = one_hot(NODES, receiver[:, part])
    index = sender[part].reshape(1, size)
    pre = nn(table, one_hot(GRID, index)) + nn(rest[:, :NODES], hot) + nn(rest[:, NODES:], feature_rows(feature[:, part]))
    return nt(hot, messages_t(pre, wt))


def slots_to_rows(row, first):
    lane = lax.broadcasted_iota(jnp.int32, (N_REG, FAR), 1)
    mine = lane // FAR_G == lax.broadcasted_iota(jnp.int32, (N_REG, FAR), 0)
    lane = lax.broadcasted_iota(jnp.int32, (2 * FAR_G, FAR), 1)
    pick = (lane % FAR_G + first == lax.broadcasted_iota(jnp.int32, (2 * FAR_G, FAR), 0)).astype(F32).astype(BF)
    high = jnp.where(mine, row // 32, 0).astype(F32).astype(BF)
    low = jnp.where(mine, row % 32, 0).astype(F32).astype(BF)
    return nt(high, pick) * 32.0 + nt(low, pick)


def asks_kernel(sender, m_sender, asks, *_):
    far = slots_to_rows(sender[NG:].reshape(1, FAR), 0) + slots_to_rows(m_sender[NM:].reshape(1, FAR), FAR_G)
    asks[...] = far.astype(jnp.int32)


def weights_kernel(w_send, live, w_recv, mesh, receiver, geo, w_out, *rest):
    wst, tables, wt, targets = rest[2:]
    eye = identity(D)
    wst[...] = (0.5 * nt(eye, w_send[...])).astype(BF)
    wrt = nt(eye, w_recv[...]).astype(BF)
    tables[:, :NODES] = (0.5 * nt(wrt, mesh[...])).astype(BF)
    lane = lax.broadcasted_iota(jnp.int32, (1, NEAR_G), 1)
    for q in range(3):
        part = slice(q * NEAR_G, (q + 1) * NEAR_G)
        targets[:, part] = jnp.where(lane < live[0, q], receiver[part].reshape(1, NEAR_G), -1)
    targets[:, NG:] = jnp.where(far_live(live, FAR), receiver[NG:].reshape(1, FAR), -1)
    half = 0.5 * geo[...]
    high = half.astype(BF).astype(F32)
    stacked = jnp.concatenate([high, high, half - high, jnp.zeros((4, D), F32)], axis=0)
    tables[:, NODES:] = nt(eye, stacked.astype(BF)).astype(BF)
    wt[...] = centred_t(w_out[...])


def first_edges_kernel(grid, wst, tables, sender, receiver, feature, wt, out, table):
    table[...] = nt(wst[...], grid[...]).astype(BF)
    value = encode_part(NEAR_G, HALF, table[...], tables[...], wt[...], sender, receiver, feature)
    out[...] = value.astype(BF)


def near_edges_kernel(table, wst, tables, sender, receiver, feature, wt, before, after, out):
    rest = (tables[...], wt[...], sender, receiver, feature)
    out[...] = encode_part(NEAR_G + HALF, HALF, table[...], *rest)
    for q, rows in ((0, before), (2, after)):
        side = nt(wst[...], rows[...]).astype(BF)
        value = encode_part(q * NEAR_G, HALF, side, *rest)
        out[...] += value + encode_part(q * NEAR_G + HALF, HALF, side, *rest)


def far_kernel(tables, receiver, feature, rows, wt, total, begun, out):
    part = slice(NG, NG + FAR)
    hot = one_hot(NODES, receiver[:, part])
    pre = nn(tables[:, :NODES], hot) + nn(tables[:, NODES:], feature_rows(feature[:, part])) + nt(identity(D), rows[...])
    value = total[...] + nt(hot, messages_t(pre, wt[...]))
    out[...] = (value + begun[...].astype(F32)).astype(BF)


def asked_hot(asked, first, nodes):
    row = lax.broadcasted_iota(jnp.int32, (FAR, N_REG), 0)
    spread = (row // FAR_G == lax.broadcasted_iota(jnp.int32, (FAR, N_REG), 1)).astype(F32).astype(BF)
    high = (asked // 32).astype(F32).astype(BF)
    low = (asked % 32).astype(F32).astype(BF)
    value = nn(spread, high) * 32.0 + nn(spread, low)
    lane = lax.broadcasted_iota(jnp.int32, (FAR, 2 * FAR_G), 1)
    slot = lax.broadcasted_iota(jnp.int32, (FAR, 2 * FAR_G), 0) % FAR_G
    index = jnp.sum(jnp.where(lane == slot + first, value, 0.0), axis=1, keepdims=True).astype(jnp.int32)
    node = lax.broadcasted_iota(jnp.int32, (FAR, nodes), 1)
    return (node == index).astype(F32).astype(BF)


def send_kernel(asked, table, out):
    out[...] = nt(asked_hot(asked[...], 0, GRID), table[...]).astype(BF)


def norm(values):
    center = values - jnp.mean(values, axis=-1, keepdims=True)
    spread = jnp.mean(center * center, axis=-1, keepdims=True)
    return center * lax.rsqrt(spread + EPSILON)


def silu(values):
    half = 0.5 * values
    return (half * jnp.tanh(half) + half).astype(BF)


def mlp(latent, summed, w_first, w_second, gain):
    merged = nn(latent, w_first[:D, :]) + nn(summed, w_first[D:, :])
    update = norm(nn(silu(merged), w_second[...])) * gain[...]
    return (latent.astype(F32) + update).astype(BF)


def plus(a, b):
    return a[...].astype(F32) + b[...].astype(F32)


def add_kernel(a, b, out):
    out[...] = plus(a, b).astype(BF)


def band_total(a, b, edge_gain):
    return (plus(a, b) * edge_gain[...]).astype(BF)


def node_kernel(asked, mesh, p0, p1, edge_gain, w_first, w_second, gain, wst, wrt, mid, rows, sent, pt):
    value = mlp(mesh[...], band_total(p0, p1, edge_gain), w_first, w_second, gain)
    table = nt(wst[...], value).astype(BF)
    sent[...] = table
    rows[...] = nn(asked_hot(asked[...], FAR_G, NODES), value).astype(BF)
    mid[...] = value
    pt[...] = nt(wrt[...], value).astype(BF)


def update_kernel(mid, p0, p1, edge_gain, w_first, w_second, gain, out):
    out[...] = mlp(mid[...], band_total(p0, p1, edge_gain), w_first, w_second, gain)


def grid_kernel(latent, w_first, w_second, gain, out, held, sems):
    copies = []
    for i in range(2):
        part, where = slice(i * GRID // 2, (i + 1) * GRID // 2), pl.ds(i * GRID // 2, GRID // 2)
        rows = latent[part, :]
        update = norm(nn(silu(nn(rows, w_first[...])), w_second[...])) * gain[...]
        held[part, :] = (rows.astype(F32) + update).astype(BF)
        copies.append(pltpu.make_async_copy(held.at[where, :], out.at[where, :], sems.at[i]))
        copies[-1].start()
    for copy in copies:
        copy.wait()


def rows_out(message, edge, gain, size):
    width = message.shape[1]
    eye = identity(NODES)
    parts = []
    for i in range(0, width, NODES):
        n = min(NODES, width - i)
        parts.append(nt(eye[:n, :n], message[:, i : i + n]))
    value = parts[0] if len(parts) == 1 else jnp.concatenate(parts, axis=0)
    return (edge.astype(F32) + value[:size, :] * gain).astype(BF)


def edge_terms_kernel(w_edge, edge, *rest):
    near, far, held, sems = rest[-4:]
    wet = (0.5 * nt(identity(D), w_edge[...])).astype(BF)
    far[...] = nt(wet, edge[NM:, :]).astype(BF)
    copies = []
    for q in range(3):
        part = slice(q * NM_PAD, (q + 1) * NM_PAD)
        held[:, part] = nt(wet, edge[q * NEAR_M : q * NEAR_M + NM_PAD, :]).astype(BF)
        where = pl.ds(q * NM_PAD, NM_PAD)
        copies.append(pltpu.make_async_copy(held.at[:, where], near.at[:, where], sems.at[q]))
        copies[-1].start()
    for copy in copies:
        copy.wait()


def prepare_kernel(w_send, live, sender, receiver, w_recv, w_out, wst, wrt, wt, near, far):
    eye = identity(D)
    wst[...] = (0.5 * nt(eye, w_send[...])).astype(BF)
    wrt[...] = (0.5 * nt(eye, w_recv[...])).astype(BF)
    wt[...] = centred_t(w_out[...])
    lane = lax.broadcasted_iota(jnp.int32, (1, NM_PAD), 1)
    for q in range(3):
        part, put = slice(q * NEAR_M, q * NEAR_M + NM_PAD), slice(q * NM_PAD, (q + 1) * NM_PAD)
        here = (lane < live[0, q]) & (lane < NEAR_M)
        near[0:1, put] = jnp.where(here, receiver[part].reshape(1, NM_PAD), -1)
        near[1:2, put] = sender[part].reshape(1, NM_PAD)
    far[...] = jnp.where(far_live(live, FAR), receiver[NM:].reshape(1, FAR), -1)


def near_kernel(edge_pre, before, own, after, index, pt, wt, total, sent, held, base, sem):
    target = index[0:1, :]
    hot = one_hot(NODES, target)
    gathered = [
        nn(table[...], one_hot(NODES, index[1:2, q * NM_PAD : (q + 1) * NM_PAD]))
        for q, table in enumerate((before, own, after))
    ]
    base[...] = nn(pt[...], hot) + jnp.concatenate(gathered, axis=1)
    message = messages_t(base[...] + edge_pre[...].astype(F32), wt[...], target >= 0)
    held[...] = message
    copy = pltpu.make_async_copy(held, sent, sem)
    copy.start()
    total[...] = nt(hot, message)
    copy.wait()


def last_kernel(target, pt, edge_pre, wst, rows, wt, total, *rest):
    out, sent = rest[-2:]
    hot = one_hot(NODES, target[...])
    pre = edge_pre[...].astype(F32) + nn(pt[...], hot) + nt(wst[...], rows[...])
    message = messages_t(pre, wt[...], target[...] >= 0)
    sent[...] = message
    out[...] = (total[...] + nt(hot, message)).astype(BF)


def edge_kernel(far, edge, near, gain, *rest):
    out, held, sem = rest[-3:]
    copies = []
    for q in (3, 0, 1, 2):
        size = NEAR_M if q < 3 else FAR
        part = slice(q * NEAR_M, q * NEAR_M + size)
        message = near[:, q * NM_PAD : (q + 1) * NM_PAD] if q < 3 else far[...]
        held[part, :] = rows_out(message, edge[part, :], gain[...], size)
        rows = pl.ds(q * NEAR_M, size)
        copies.append(pltpu.make_async_copy(held.at[rows, :], out.at[rows, :], sem.at[q]))
        copies[-1].start()
    for copy in copies:
        copy.wait()


def swap(x, even, odd):
    regions = lax.axis_size("region")
    pairs = [
        (band * regions + region, (band ^ (odd if region % 2 else even)) * regions + region)
        for band in range(lax.axis_size("band"))
        for region in range(regions)
    ]
    return lax.ppermute(x, ("band", "region"), pairs)


def band_stages(part, first_args, first):
    part, first_args = lax.optimization_barrier((part, first_args))
    part_in = swap(part, 1, 3)
    first_out = first(first_args)
    part_in, first_out = lax.optimization_barrier((part_in, first_out))
    part = call(add_kernel, [kept((NODES, D), BF)], "VV", (part, part_in), name="band_add")
    return part, swap(part, 3, 1), first_out


def halo(x):
    count = lax.axis_size("region")
    up = [(i, (i + 1) % count) for i in range(count)]
    down = [(j, i) for i, j in up]
    return lax.ppermute(x, "region", up), lax.ppermute(x, "region", down)


def exchange(x):
    return lax.all_to_all(x, "region", split_axis=0, concat_axis=0, tiled=True)


def on_device(
    grid_latent,
    mesh_latent,
    encode_sender,
    encode_receiver,
    encode_live,
    encode_feature,
    mesh_edge,
    mesh_sender,
    mesh_receiver,
    mesh_live,
    grid_first,
    grid_second,
    grid_gain,
    encode_send,
    encode_receive,
    encode_geometry,
    encode_output,
    encode_gain,
    node_first,
    node_second,
    node_gain,
    process_edge,
    process_send,
    process_receive,
    process_output,
    process_gain,
    update_first,
    update_second,
    update_gain,
):
    gains = [g.reshape(1, D) for g in (grid_gain, encode_gain, node_gain, process_gain, update_gain)]
    before, after = halo(grid_latent)
    weight = kept((D, D), BF)
    asks, sender = call(
        asks_kernel,
        [kept((N_REG, 2 * FAR_G), jnp.int32)],
        "KH",
        (encode_sender, mesh_sender),
        name="far_asks",
    )
    asked = exchange(asks)
    asks_sent, w_send = lax.optimization_barrier((asks, encode_send))
    wst, tables, wt, receiver, grid, feature = call(
        weights_kernel,
        (weight, kept((D, NODES + 16), BF), weight, kept((1, NG + FAR), jnp.int32)),
        "HSHHHHHKK",
        (w_send, encode_live, encode_receive, mesh_latent, encode_receiver, encode_geometry, encode_output)
        + (grid_latent, encode_feature),
        flops=3 * 10**9,
        name="encode_weights",
        grant=56,
    )
    begun, table = call(
        first_edges_kernel,
        (kept((NODES, D), BF), kept((D, GRID), BF)),
        "VVVVVVV",
        (grid, wst, tables, sender, receiver, feature, wt),
        flops=3 * 10**9,
        name="encode_begin",
        grant=56,
    )
    asked, table = lax.optimization_barrier((asked, table))
    outgoing = call(send_kernel, [shape((FAR, D), BF)], "VV", (asked, table), flops=3 * 10**8, name="encode_rows")
    far_rows = exchange(outgoing.reshape(N_REG, FAR_G, D)).reshape(FAR, D)
    outgoing, table = lax.optimization_barrier((outgoing, table))
    total = call(
        near_edges_kernel,
        [kept((NODES, D), F32)],
        "VVVVVVVHH",
        (table, wst, tables, sender, receiver, feature, wt, before, after),
        flops=15 * 10**9,
        name="encode_near",
        grant=56,
    )
    part = call(
        far_kernel,
        [kept((NODES, D), BF)],
        "VVVVVVH",
        (tables, receiver, feature, far_rows, wt, total, begun),
        flops=10**9,
        name="encode_far",
        grant=56,
    )

    def edge_terms(args):
        return call(
            edge_terms_kernel,
            (pltpu.HBM((D, 3 * NM_PAD), BF), kept((D, FAR), BF)),
            "HHKKKKKKKKKK",
            args,
            scratch=[pltpu.VMEM((D, 3 * NM_PAD), BF), pltpu.SemaphoreType.DMA((3,))],
            out_specs=(HBM, VMEM),
            flops=2 * 10**9,
            name="process_terms",
        )

    def prepare(args):
        return call(
            prepare_kernel,
            (weight, weight, weight, kept((8, 3 * NM_PAD), jnp.int32), kept((1, FAR), jnp.int32)),
            "VSVVVV",
            args,
            flops=2 * 10**9,
            name="process_prepare",
        )

    part, part_in, terms = band_stages(
        part,
        (process_edge, mesh_edge, process_send, mesh_sender, mesh_receiver, process_receive, process_output)
        + (node_first, node_second, mesh_latent, gains[1], gains[2]),
        edge_terms,
    )
    near_pre, far_pre, p_send, p_from, p_to, p_recv, p_out, n_first, n_second, n_mesh, n_eg, n_gain = terms
    part, p_send = lax.optimization_barrier((part, p_send))
    p_wst, p_wrt, p_wt, near_index, far_index = prepare((p_send, mesh_live, p_from, p_to, p_recv, p_out))
    mid, rows, own_table, pt = call(
        node_kernel,
        (kept((NODES, D), BF), shape((FAR, D), BF), kept((D, NODES), BF), kept((D, NODES), BF)),
        "VVVVVVVVVV",
        (asked, n_mesh, part, part_in, n_eg, n_first, n_second, n_gain, p_wst, p_wrt),
        flops=10**9,
        name="mesh_nodes",
    )
    far_mesh = exchange(rows.reshape(N_REG, FAR_M, D)).reshape(FAR, D)
    before_table, after_table = halo(own_table)
    m_total, near_sent = call(
        near_kernel,
        (kept((NODES, D), F32), pltpu.HBM((D, 3 * NM_PAD), BF)),
        "HVVVVVV",
        (near_pre, before_table, own_table, after_table, near_index, pt, p_wt),
        scratch=[pltpu.VMEM((D, 3 * NM_PAD), kind) for kind in (BF, F32)] + [pltpu.SemaphoreType.DMA],
        out_specs=(VMEM, HBM),
        flops=4 * 10**9,
        name="process_near",
    )
    part, far_sent = call(
        last_kernel,
        (kept((NODES, D), BF), kept((D, FAR), BF)),
        "VVVVVVV",
        (far_index, pt, far_pre, p_wst, far_mesh, p_wt, m_total),
        flops=10**9,
        name="process_far",
    )

    def edge_rows(args):
        return call(
            edge_kernel,
            [pltpu.HBM((M2M, D), BF)],
            "VHHKKKKKKKK",
            args,
            scratch=[pltpu.VMEM((M2M, D), BF), pltpu.SemaphoreType.DMA((4,))],
            out_specs=[HBM],
            flops=3 * 10**9,
            name="process_rows",
        )

    part, part_in, from_rows = band_stages(
        part,
        (far_sent, mesh_edge, near_sent, gains[3], grid_latent, grid_first, grid_second, gains[0])
        + (update_first, update_second, gains[4]),
        edge_rows,
    )
    edge_out, m_gain, g_rows, g_first, g_second, g_gain, u_first, u_second, u_gain = from_rows
    part, g_rows = lax.optimization_barrier((part, g_rows))
    grid_out = call(
        grid_kernel,
        [pltpu.HBM((GRID, D), BF)],
        "VVVV",
        (g_rows, g_first, g_second, g_gain),
        scratch=[pltpu.VMEM((GRID, D), BF), pltpu.SemaphoreType.DMA((2,))],
        out_specs=[HBM],
        flops=3 * 10**9,
        name="grid_nodes",
    )
    grid_out, u_gain = lax.optimization_barrier((grid_out, u_gain))
    mesh_out = call(
        update_kernel,
        [shape((NODES, D), BF)],
        "VVVVVVV",
        (mid, part, part_in, m_gain, u_first, u_second, u_gain),
        flops=10**9,
        name="mesh_update",
    )
    return (grid_out, mesh_out, edge_out)


def solution(mesh):
    edge = P(("band", "region"))
    rows = P(("band", "region"), None)
    mesh_rows = P("region", None)
    return jax.shard_map(
        on_device,
        mesh=mesh,
        in_specs=(rows, mesh_rows, edge, edge, rows, P(None, ("band", "region")), rows, edge, edge, rows) + (P(),) * 19,
        out_specs=(rows, mesh_rows, rows),
        check_vma=False,
    )
```

```python
import functools

import jax
import jax.numpy as jnp
from jax import lax
from jax.experimental import pallas as pl
from jax.experimental.pallas import tpu as pltpu
from jax.sharding import PartitionSpec as P

NEAR_G = 2048
FAR_G = 8
NEAR_M = 576
FAR_M = 8
EPSILON = 1e-05
D = 512
NODES = 256
GRID = 1024
N_REG = 32
FAR = N_REG * FAR_G
NG = 3 * NEAR_G
NM = 3 * NEAR_M
NM_PAD = 640
M2M = NM + FAR
BF = jnp.bfloat16
F32 = jnp.float32
VMEM = pl.BlockSpec(memory_space=pltpu.VMEM)
SMEM = pl.BlockSpec(memory_space=pltpu.SMEM)
ANY = pl.BlockSpec(memory_space=pl.ANY)
HBM = pl.BlockSpec(memory_space=pltpu.HBM)
HALF = NEAR_G // 2


def nt(a, b):
    return lax.dot_general(a, b, (((1,), (1,)), ((), ())), preferred_element_type=F32)


def nn(a, b):
    return jnp.dot(a, b, preferred_element_type=F32)


def identity(n):
    row = lax.broadcasted_iota(jnp.int32, (n, n), 0)
    return (row == lax.broadcasted_iota(jnp.int32, (n, n), 1)).astype(F32).astype(BF)


def one_hot(rows, index):
    row = lax.broadcasted_iota(jnp.int32, (rows, index.shape[1]), 0).astype(jnp.int16)
    return jnp.where(row == index.astype(jnp.int16), jnp.ones((), BF), jnp.zeros((), BF))


def centred_t(weight):
    w_t = nt(identity(D), weight)
    return (w_t - jnp.mean(w_t, axis=0, keepdims=True)).astype(BF)


def feature_rows(feature):
    high = feature.astype(BF).astype(F32)
    zero = jnp.zeros(feature.shape, F32)
    return jnp.concatenate([high, feature - high, high, zero], axis=0).astype(BF)


def messages_t(half_pre, w_out_t, live=None):
    hidden = (half_pre * jnp.tanh(half_pre) + half_pre).astype(BF)
    y = nn(w_out_t, hidden)
    spread = jnp.sum(y * y, axis=0, keepdims=True) * (1 / D)
    scale = lax.rsqrt(spread + EPSILON)
    if live is not None:
        scale = jnp.where(live, scale, 0.0)
    return (y * scale).astype(BF)


def far_live(counts, width):
    lane = lax.broadcasted_iota(jnp.int32, (1, width), 1)
    limit = jnp.zeros((1, width), jnp.int32)
    for k in range(N_REG):
        limit = jnp.where(lane // FAR_G == k, counts[0, 3 + k], limit)
    return lane % FAR_G < limit


class Late:
    def __init__(self, held, copy):
        self.held, self.copy = held, copy
        self.shape = held.shape

    def __getitem__(self, index):
        if self.copy is not None:
            self.copy.wait()
            self.copy = None
        return self.held[index]


def call(kernel, outs, specs, args, scratch=(), out_specs=None, flops=0, name=None, aliases=None, grant=24):
    outs = jax.tree.leaves(outs)
    scratch_in = [i for i, spec in enumerate(specs) if spec in "SHF"]
    keep = [i for i, spec in enumerate(specs) if spec == "K"]
    late = scratch_in + keep
    n_in, n_out, n_keep = len(args), len(outs), len(keep)
    place = {"S": HBM, "H": HBM, "K": HBM, "F": HBM, "V": VMEM, "R": ANY}
    pin = {"S": pltpu.HBM, "H": pltpu.HBM, "K": pltpu.HBM, "F": pltpu.HBM, "V": pltpu.VMEM, "R": pl.ANY}

    def body(*refs):
        ins, rest = list(refs[:n_in]), refs[n_in:]
        targets = list(rest[n_out + n_keep : n_out + n_keep + len(scratch_in)]) + list(rest[n_out : n_out + n_keep])
        rest_scratch = rest[n_out + n_keep + len(scratch_in) :]
        if late:
            sems, rest_scratch = rest_scratch[0], rest_scratch[1:]
        order = sorted(range(len(late)), key=lambda j: late[j])
        for j in order:
            source = ins[late[j]].at[pl.ds(NM, FAR), :] if specs[late[j]] == "F" else ins[late[j]]
            copy = pltpu.make_async_copy(source, targets[j], sems.at[j])
            copy.start()
            ins[late[j]] = Late(targets[j], copy)
        kernel(*ins, *rest[:n_out], *rest_scratch)
        for i in late:
            if ins[i].copy is not None:
                ins[i].copy.wait()

    out_shape = outs + [pltpu.VMEM(args[i].shape, args[i].dtype) for i in keep]
    result = pl.pallas_call(
        body,
        out_shape=out_shape,
        in_specs=[place[spec] for spec in specs],
        out_specs=(list(out_specs) if out_specs else [VMEM] * n_out) + [VMEM] * n_keep,
        scratch_shapes=[
            pltpu.VMEM((FAR, D), BF)
            if specs[i] == "F"
            else (pltpu.SMEM if specs[i] == "S" else pltpu.VMEM)(args[i].shape, args[i].dtype)
            for i in scratch_in
        ]
        + ([pltpu.SemaphoreType.DMA((len(late),))] if late else [])
        + list(scratch),
        compiler_params=pltpu.CompilerParams(vmem_limit_bytes=grant * 2**20),
        cost_estimate=pl.CostEstimate(flops=flops, bytes_accessed=2**20, transcendentals=0),
        input_output_aliases=aliases or {},
        name=name,
    )(*[arg if spec == "R" else pltpu.with_memory_space_constraint(arg, pin[spec]) for arg, spec in zip(args, specs)])
    return result if len(result) > 1 else result[0]


def shape(dims, kind):
    return jax.ShapeDtypeStruct(dims, kind)


def kept(dims, kind):
    return pltpu.VMEM(dims, kind)


def encode_part(begin, size, table, rest, wt, sender, receiver, feature):
    part = slice(begin, begin + size)
    hot = one_hot(NODES, receiver[:, part])
    index = sender[part].reshape(1, size)
    pre = nn(table, one_hot(GRID, index)) + nn(rest[:, :NODES], hot) + nn(rest[:, NODES:], feature_rows(feature[:, part]))
    return nt(hot, messages_t(pre, wt))


def slots_to_rows(row, first):
    lane = lax.broadcasted_iota(jnp.int32, (N_REG, FAR), 1)
    mine = lane // FAR_G == lax.broadcasted_iota(jnp.int32, (N_REG, FAR), 0)
    lane = lax.broadcasted_iota(jnp.int32, (2 * FAR_G, FAR), 1)
    pick = (lane % FAR_G + first == lax.broadcasted_iota(jnp.int32, (2 * FAR_G, FAR), 0)).astype(F32).astype(BF)
    high = jnp.where(mine, row // 32, 0).astype(F32).astype(BF)
    low = jnp.where(mine, row % 32, 0).astype(F32).astype(BF)
    return nt(high, pick) * 32.0 + nt(low, pick)


def asks_kernel(sender, m_sender, asks, *_):
    far = slots_to_rows(sender[NG:].reshape(1, FAR), 0) + slots_to_rows(m_sender[NM:].reshape(1, FAR), FAR_G)
    asks[...] = far.astype(jnp.int32)


def weights_kernel(w_send, live, w_recv, mesh, receiver, geo, w_out, *rest):
    wst, tables, wt, targets = rest[2:]
    eye = identity(D)
    wst[...] = (0.5 * nt(eye, w_send[...])).astype(BF)
    wrt = nt(eye, w_recv[...]).astype(BF)
    tables[:, :NODES] = (0.5 * nt(wrt, mesh[...])).astype(BF)
    lane = lax.broadcasted_iota(jnp.int32, (1, NEAR_G), 1)
    for q in range(3):
        part = slice(q * NEAR_G, (q + 1) * NEAR_G)
        targets[:, part] = jnp.where(lane < live[0, q], receiver[part].reshape(1, NEAR_G), -1)
    targets[:, NG:] = jnp.where(far_live(live, FAR), receiver[NG:].reshape(1, FAR), -1)
    half = 0.5 * geo[...]
    high = half.astype(BF).astype(F32)
    stacked = jnp.concatenate([high, high, half - high, jnp.zeros((4, D), F32)], axis=0)
    tables[:, NODES:] = nt(eye, stacked.astype(BF)).astype(BF)
    wt[...] = centred_t(w_out[...])


def first_edges_kernel(grid, wst, tables, sender, receiver, feature, wt, out, table):
    table[...] = nt(wst[...], grid[...]).astype(BF)
    value = encode_part(NEAR_G, HALF, table[...], tables[...], wt[...], sender, receiver, feature)
    out[...] = value.astype(BF)


def near_edges_kernel(table, wst, tables, sender, receiver, feature, wt, before, after, out):
    rest = (tables[...], wt[...], sender, receiver, feature)
    out[...] = encode_part(NEAR_G + HALF, HALF, table[...], *rest)
    for q, rows in ((0, before), (2, after)):
        side = nt(wst[...], rows[...]).astype(BF)
        value = encode_part(q * NEAR_G, HALF, side, *rest)
        out[...] += value + encode_part(q * NEAR_G + HALF, HALF, side, *rest)


def far_kernel(tables, receiver, feature, rows, wt, total, begun, out):
    part = slice(NG, NG + FAR)
    hot = one_hot(NODES, receiver[:, part])
    pre = nn(tables[:, :NODES], hot) + nn(tables[:, NODES:], feature_rows(feature[:, part])) + nt(identity(D), rows[...])
    value = total[...] + nt(hot, messages_t(pre, wt[...]))
    out[...] = (value + begun[...].astype(F32)).astype(BF)


def asked_hot(asked, first, nodes):
    row = lax.broadcasted_iota(jnp.int32, (FAR, N_REG), 0)
    spread = (row // FAR_G == lax.broadcasted_iota(jnp.int32, (FAR, N_REG), 1)).astype(F32).astype(BF)
    high = (asked // 32).astype(F32).astype(BF)
    low = (asked % 32).astype(F32).astype(BF)
    value = nn(spread, high) * 32.0 + nn(spread, low)
    lane = lax.broadcasted_iota(jnp.int32, (FAR, 2 * FAR_G), 1)
    slot = lax.broadcasted_iota(jnp.int32, (FAR, 2 * FAR_G), 0) % FAR_G
    index = jnp.sum(jnp.where(lane == slot + first, value, 0.0), axis=1, keepdims=True).astype(jnp.int32)
    node = lax.broadcasted_iota(jnp.int32, (FAR, nodes), 1)
    return (node == index).astype(F32).astype(BF)


def send_kernel(asked, table, out):
    out[...] = nt(asked_hot(asked[...], 0, GRID), table[...]).astype(BF)


def norm(values):
    center = values - jnp.mean(values, axis=-1, keepdims=True)
    spread = jnp.mean(center * center, axis=-1, keepdims=True)
    return center * lax.rsqrt(spread + EPSILON)


def silu(values):
    half = 0.5 * values
    return (half * jnp.tanh(half) + half).astype(BF)


def mlp(latent, base, summed, w_first, w_second, gain):
    merged = base[...] + nn(summed, w_first[D:, :])
    update = norm(nn(silu(merged), w_second[...])) * gain[...]
    return (latent.astype(F32) + update).astype(BF)


def plus(a, b):
    return a[...].astype(F32) + b[...].astype(F32)


def add_kernel(a, b, out):
    out[...] = plus(a, b).astype(BF)


def band_total(a, b, edge_gain):
    return (plus(a, b) * edge_gain[...]).astype(BF)


def node_kernel(hot, base, mesh, p0, p1, edge_gain, w_first, w_second, gain, wst, wrt, mid, rows, sent, pt):
    value = mlp(mesh[...], base, band_total(p0, p1, edge_gain), w_first, w_second, gain)
    table = nt(wst[...], value).astype(BF)
    sent[...] = table
    rows[...] = nn(hot[...], value).astype(BF)
    mid[...] = value
    pt[...] = nt(wrt[...], value).astype(BF)


def update_kernel(mid, base, p0, p1, edge_gain, w_first, w_second, gain, out):
    out[...] = mlp(mid[...], base, band_total(p0, p1, edge_gain), w_first, w_second, gain)


def grid_kernel(latent, w_first, w_second, gain, mid, u_first, out, base, held, sems):
    base[...] = nn(mid[...], u_first[:D, :])
    copies = []
    for i in range(2):
        part, where = slice(i * GRID // 2, (i + 1) * GRID // 2), pl.ds(i * GRID // 2, GRID // 2)
        rows = latent[part, :]
        update = norm(nn(silu(nn(rows, w_first[...])), w_second[...])) * gain[...]
        held[part, :] = (rows.astype(F32) + update).astype(BF)
        copies.append(pltpu.make_async_copy(held.at[where, :], out.at[where, :], sems.at[i]))
        copies[-1].start()
    for copy in copies:
        copy.wait()


def rows_out(message, edge, gain, size):
    width = message.shape[1]
    eye = identity(NODES)
    parts = []
    for i in range(0, width, NODES):
        n = min(NODES, width - i)
        parts.append(nt(eye[:n, :n], message[:, i : i + n]))
    value = parts[0] if len(parts) == 1 else jnp.concatenate(parts, axis=0)
    return (edge.astype(F32) + value[:size, :] * gain).astype(BF)


def edge_terms_kernel(w_edge, edge, *rest):
    near, far, held, sems = rest[-4:]
    wet = (0.5 * nt(identity(D), w_edge[...])).astype(BF)
    far[...] = nt(wet, edge[NM:, :]).astype(BF)
    copies = []
    for q in range(3):
        part = slice(q * NM_PAD, (q + 1) * NM_PAD)
        held[:, part] = nt(wet, edge[q * NEAR_M : q * NEAR_M + NM_PAD, :]).astype(BF)
        where = pl.ds(q * NM_PAD, NM_PAD)
        copies.append(pltpu.make_async_copy(held.at[:, where], near.at[:, where], sems.at[q]))
        copies[-1].start()
    for copy in copies:
        copy.wait()


def prepare_kernel(
    w_send, live, sender, receiver, w_recv, w_out, asked, mesh, n_first, wst, wrt, wt, near, far, hot, base
):
    hot[...] = asked_hot(asked[...], FAR_G, NODES)
    base[...] = nn(mesh[...], n_first[:D, :])
    eye = identity(D)
    wst[...] = (0.5 * nt(eye, w_send[...])).astype(BF)
    wrt[...] = (0.5 * nt(eye, w_recv[...])).astype(BF)
    wt[...] = centred_t(w_out[...])
    lane = lax.broadcasted_iota(jnp.int32, (1, NM_PAD), 1)
    for q in range(3):
        part, put = slice(q * NEAR_M, q * NEAR_M + NM_PAD), slice(q * NM_PAD, (q + 1) * NM_PAD)
        here = (lane < live[0, q]) & (lane < NEAR_M)
        near[0:1, put] = jnp.where(here, receiver[part].reshape(1, NM_PAD), -1)
        near[1:2, put] = sender[part].reshape(1, NM_PAD)
    far[...] = jnp.where(far_live(live, FAR), receiver[NM:].reshape(1, FAR), -1)


def near_kernel(edge_pre, before, own, after, index, pt, wt, total, sent, held, base, sem):
    target = index[0:1, :]
    hot = one_hot(NODES, target)
    gathered = [
        nn(table[...], one_hot(NODES, index[1:2, q * NM_PAD : (q + 1) * NM_PAD]))
        for q, table in enumerate((before, own, after))
    ]
    base[...] = nn(pt[...], hot) + jnp.concatenate(gathered, axis=1)
    message = messages_t(base[...] + edge_pre[...].astype(F32), wt[...], target >= 0)
    held[...] = message
    copy = pltpu.make_async_copy(held, sent, sem)
    copy.start()
    total[...] = nt(hot, message)
    copy.wait()


def last_kernel(target, pt, edge_pre, wst, rows, wt, total, *rest):
    out, sent = rest[-2:]
    hot = one_hot(NODES, target[...])
    pre = edge_pre[...].astype(F32) + nn(pt[...], hot) + nt(wst[...], rows[...])
    message = messages_t(pre, wt[...], target[...] >= 0)
    sent[...] = message
    out[...] = (total[...] + nt(hot, message)).astype(BF)


def edge_kernel(far, edge, near, gain, *rest):
    out, held, sem = rest[-3:]
    copies = []
    for q in (3, 0, 1, 2):
        size = NEAR_M if q < 3 else FAR
        part = slice(q * NEAR_M, q * NEAR_M + size)
        message = near[:, q * NM_PAD : (q + 1) * NM_PAD] if q < 3 else far[...]
        held[part, :] = rows_out(message, edge[part, :], gain[...], size)
        rows = pl.ds(q * NEAR_M, size)
        copies.append(pltpu.make_async_copy(held.at[rows, :], out.at[rows, :], sem.at[q]))
        copies[-1].start()
    for copy in copies:
        copy.wait()


def swap(x, even, odd):
    regions = lax.axis_size("region")
    pairs = [
        (band * regions + region, (band ^ (odd if region % 2 else even)) * regions + region)
        for band in range(lax.axis_size("band"))
        for region in range(regions)
    ]
    return lax.ppermute(x, ("band", "region"), pairs)


def band_stages(part, first_args, first):
    part, first_args = lax.optimization_barrier((part, first_args))
    part_in = swap(part, 1, 3)
    first_out = first(first_args)
    part_in, first_out = lax.optimization_barrier((part_in, first_out))
    part = call(add_kernel, [kept((NODES, D), BF)], "VV", (part, part_in), name="band_add")
    return part, swap(part, 3, 1), first_out


def halo(x):
    count = lax.axis_size("region")
    up = [(i, (i + 1) % count) for i in range(count)]
    down = [(j, i) for i, j in up]
    return lax.ppermute(x, "region", up), lax.ppermute(x, "region", down)


def exchange(x):
    return lax.all_to_all(x, "region", split_axis=0, concat_axis=0, tiled=True)


def on_device(
    grid_latent,
    mesh_latent,
    encode_sender,
    encode_receiver,
    encode_live,
    encode_feature,
    mesh_edge,
    mesh_sender,
    mesh_receiver,
    mesh_live,
    grid_first,
    grid_second,
    grid_gain,
    encode_send,
    encode_receive,
    encode_geometry,
    encode_output,
    encode_gain,
    node_first,
    node_second,
    node_gain,
    process_edge,
    process_send,
    process_receive,
    process_output,
    process_gain,
    update_first,
    update_second,
    update_gain,
):
    gains = [g.reshape(1, D) for g in (grid_gain, encode_gain, node_gain, process_gain, update_gain)]
    before, after = halo(grid_latent)
    weight = kept((D, D), BF)
    asks, sender = call(
        asks_kernel,
        [kept((N_REG, 2 * FAR_G), jnp.int32)],
        "KH",
        (encode_sender, mesh_sender),
        name="far_asks",
    )
    asked = exchange(asks)
    asks_sent, w_send = lax.optimization_barrier((asks, encode_send))
    wst, tables, wt, receiver, grid, feature = call(
        weights_kernel,
        (weight, kept((D, NODES + 16), BF), weight, kept((1, NG + FAR), jnp.int32)),
        "HSHHHHHKK",
        (w_send, encode_live, encode_receive, mesh_latent, encode_receiver, encode_geometry, encode_output)
        + (grid_latent, encode_feature),
        flops=3 * 10**9,
        name="encode_weights",
        grant=56,
    )
    begun, table = call(
        first_edges_kernel,
        (kept((NODES, D), BF), kept((D, GRID), BF)),
        "VVVVVVV",
        (grid, wst, tables, sender, receiver, feature, wt),
        flops=3 * 10**9,
        name="encode_begin",
        grant=56,
    )
    asked, table = lax.optimization_barrier((asked, table))
    outgoing = call(send_kernel, [shape((FAR, D), BF)], "VV", (asked, table), flops=3 * 10**8, name="encode_rows")
    far_rows = exchange(outgoing.reshape(N_REG, FAR_G, D)).reshape(FAR, D)
    outgoing, table = lax.optimization_barrier((outgoing, table))
    total = call(
        near_edges_kernel,
        [kept((NODES, D), F32)],
        "VVVVVVVHH",
        (table, wst, tables, sender, receiver, feature, wt, before, after),
        flops=15 * 10**9,
        name="encode_near",
        grant=56,
    )
    part = call(
        far_kernel,
        [kept((NODES, D), BF)],
        "VVVVVVH",
        (tables, receiver, feature, far_rows, wt, total, begun),
        flops=10**9,
        name="encode_far",
        grant=56,
    )

    def edge_terms(args):
        return call(
            edge_terms_kernel,
            (pltpu.HBM((D, 3 * NM_PAD), BF), kept((D, FAR), BF)),
            "HHKKKKKKKKKK",
            args,
            scratch=[pltpu.VMEM((D, 3 * NM_PAD), BF), pltpu.SemaphoreType.DMA((3,))],
            out_specs=(HBM, VMEM),
            flops=2 * 10**9,
            name="process_terms",
        )

    def prepare(args):
        return call(
            prepare_kernel,
            (weight, weight, weight, kept((8, 3 * NM_PAD), jnp.int32), kept((1, FAR), jnp.int32))
            + (kept((FAR, NODES), BF), kept((NODES, D), F32)),
            "VSVVVVVVV",
            args,
            flops=2 * 10**9,
            name="process_prepare",
        )

    part, part_in, terms = band_stages(
        part,
        (process_edge, mesh_edge, process_send, mesh_sender, mesh_receiver, process_receive, process_output)
        + (node_first, node_second, mesh_latent, gains[1], gains[2]),
        edge_terms,
    )
    near_pre, far_pre, p_send, p_from, p_to, p_recv, p_out, n_first, n_second, n_mesh, n_eg, n_gain = terms
    part, p_send = lax.optimization_barrier((part, p_send))
    p_wst, p_wrt, p_wt, near_index, far_index, n_hot, n_base = prepare(
        (p_send, mesh_live, p_from, p_to, p_recv, p_out, asked, n_mesh, n_first)
    )
    mid, rows, own_table, pt = call(
        node_kernel,
        (kept((NODES, D), BF), shape((FAR, D), BF), kept((D, NODES), BF), kept((D, NODES), BF)),
        "VVVVVVVVVVV",
        (n_hot, n_base, n_mesh, part, part_in, n_eg, n_first, n_second, n_gain, p_wst, p_wrt),
        flops=10**9,
        name="mesh_nodes",
    )
    far_mesh = exchange(rows.reshape(N_REG, FAR_M, D)).reshape(FAR, D)
    before_table, after_table = halo(own_table)
    m_total, near_sent = call(
        near_kernel,
        (kept((NODES, D), F32), pltpu.HBM((D, 3 * NM_PAD), BF)),
        "HVVVVVV",
        (near_pre, before_table, own_table, after_table, near_index, pt, p_wt),
        scratch=[pltpu.VMEM((D, 3 * NM_PAD), kind) for kind in (BF, F32)] + [pltpu.SemaphoreType.DMA],
        out_specs=(VMEM, HBM),
        flops=4 * 10**9,
        name="process_near",
    )
    part, far_sent = call(
        last_kernel,
        (kept((NODES, D), BF), kept((D, FAR), BF)),
        "VVVVVVV",
        (far_index, pt, far_pre, p_wst, far_mesh, p_wt, m_total),
        flops=10**9,
        name="process_far",
    )

    def edge_rows(args):
        return call(
            edge_kernel,
            [pltpu.HBM((M2M, D), BF)],
            "VHHKKKKKKKK",
            args,
            scratch=[pltpu.VMEM((M2M, D), BF), pltpu.SemaphoreType.DMA((4,))],
            out_specs=[HBM],
            flops=3 * 10**9,
            name="process_rows",
        )

    part, part_in, from_rows = band_stages(
        part,
        (far_sent, mesh_edge, near_sent, gains[3], grid_latent, grid_first, grid_second, gains[0])
        + (update_first, update_second, gains[4]),
        edge_rows,
    )
    edge_out, m_gain, g_rows, g_first, g_second, g_gain, u_first, u_second, u_gain = from_rows
    part, g_rows = lax.optimization_barrier((part, g_rows))
    grid_out, u_base = call(
        grid_kernel,
        [pltpu.HBM((GRID, D), BF), kept((NODES, D), F32)],
        "VVVVVV",
        (g_rows, g_first, g_second, g_gain, mid, u_first),
        scratch=[pltpu.VMEM((GRID, D), BF), pltpu.SemaphoreType.DMA((2,))],
        out_specs=[HBM, VMEM],
        flops=3 * 10**9,
        name="grid_nodes",
    )
    grid_out, u_gain = lax.optimization_barrier((grid_out, u_gain))
    mesh_out = call(
        update_kernel,
        [shape((NODES, D), BF)],
        "VVVVVVVV",
        (mid, u_base, part, part_in, m_gain, u_first, u_second, u_gain),
        flops=10**9,
        name="mesh_update",
    )
    return (grid_out, mesh_out, edge_out)


def solution(mesh):
    edge = P(("band", "region"))
    rows = P(("band", "region"), None)
    mesh_rows = P("region", None)
    return jax.shard_map(
        on_device,
        mesh=mesh,
        in_specs=(rows, mesh_rows, edge, edge, rows, P(None, ("band", "region")), rows, edge, edge, rows) + (P(),) * 19,
        out_specs=(rows, mesh_rows, rows),
        check_vma=False,
    )
```
